512 devices in a mesh: grp: 8 (over y), reply: 16 (over x, z_lo), head: 4 (over z_hi, core).
Axes of the slice: x: 4, y: 8, z: 8 (z_hi: 2, z_lo: 4; z = z_hi * 4 + z_lo), core: 2. Of those that a mesh axis runs over, the one named last changes fastest.
Arguments:
- queries: bfloat16 [8, 16, 256, 4096], P('grp', 'reply', None, 'head'), may hold values from -4.5 to 4.5
- reply_kv: bfloat16 [8, 16, 2, 256, 512], P('grp', 'reply', None, None, 'head'), may hold values from -6 to 6
- prompt_kv: bfloat16 [8, 2, 1024, 512], P('grp', None, 'reply', 'head'), may hold values from -4.5 to 4.5
- saved_out: bfloat16 [8, 16, 256, 4096], P('grp', 'reply', None, 'head'), may hold values from -6 to 6
- grad_out: bfloat16 [8, 16, 256, 4096], P('grp', 'reply', None, 'head'), may hold values from -6 to 6
- prompt_len: int32 [8], P('grp'), may hold values from 128 to 1024
- reply_len: int32 [8, 16], P('grp', 'reply'), may hold values from 1 to 256, as said below
Outputs:
- query_grad: bfloat16 [8, 16, 256, 4096], P('grp', 'reply', None, 'head')
- reply_kv_grad: bfloat16 [8, 16, 2, 256, 512], P('grp', 'reply', None, None, 'head')
- prompt_kv_grad: bfloat16 [8, 2, 1024, 512], P('grp', None, 'reply', 'head')
- value_bias_grad: float32 [512], P('head')
The draws below stay inside these ranges and needn't reach their ends.
Inputs may be any that keep to these rules, and one draw needn't show every extreme that they name: `reply_len`: live tokens of each reply; every group has a reply of 256 tokens.
All inputs are finite; a program needn't handle non-finite values.
Results may differ from the reference program's by a relative error of at most 0.0049.
Values may be sent and summed in bfloat16 or wider, within the bound.
A program may use at most 64 MiB of HBM per device.

```python
import jax
import jax.numpy as jnp
from jax import lax

HD = 128
QPK = 8
RLEN = 256
PMAX = 1024
KV_HEADS = 4
Q_HEADS = 32
GROUPS = 8
REPLIES = 16


def draw_queries(key, part):
    key = jax.random.fold_in(key, 11)
    shape = (GROUPS, REPLIES, RLEN, KV_HEADS, QPK, HD)
    base = jnp.clip(jax.random.normal(key, shape, jnp.float32), -4.5, 4.5)
    return base.reshape(GROUPS, REPLIES, RLEN, Q_HEADS * HD).astype(jnp.bfloat16)


def draw_prompt_kv(key, part):
    key = jax.random.fold_in(key, 12)
    shape = (GROUPS, 2, PMAX, KV_HEADS * HD)
    base = jnp.clip(jax.random.normal(key, shape, jnp.float32), -4.5, 4.5)
    return base.astype(jnp.bfloat16)


def draw_prompt_len(key, part):
    key = jax.random.fold_in(key, 21)
    first, second = jax.random.split(key)
    values = jax.random.randint(first, (GROUPS,), PMAX // 8, PMAX + 1, dtype=jnp.int32)
    longest = jax.random.randint(second, (), 0, GROUPS, dtype=jnp.int32)
    values = values.at[longest].set(PMAX)
    values = values.at[(longest + 1) % GROUPS].set(PMAX // 8)
    return values.astype(jnp.int32)


def draw_reply_len(key, part):
    key = jax.random.fold_in(key, 22)
    first, second, third = jax.random.split(key, 3)
    values = jax.random.randint(first, (GROUPS, REPLIES), 1, RLEN + 1, dtype=jnp.int32)
    fullest = jax.random.randint(second, (GROUPS,), 0, REPLIES, dtype=jnp.int32)
    values = values.at[jnp.arange(GROUPS, dtype=jnp.int32), fullest].set(RLEN)
    chosen = jax.random.randint(third, (), 0, GROUPS, dtype=jnp.int32)
    values = values.at[chosen, (fullest[chosen] + 1) % REPLIES].set(1)
    return values.astype(jnp.int32)


def block_scale(key, shape, cuts, least, largest):
    def one(position, parts):
        heights = jax.random.uniform(jax.random.fold_in(jax.random.fold_in(key, 6), position), (parts,), jnp.float32, least / len(cuts), largest / len(cuts))
        return jnp.repeat(jnp.exp(heights), shape[position] // parts).reshape((-1,) + (1,) * (len(shape) - position - 1))

    gain = one(*cuts[0])
    for cut in cuts[1:]:
        gain = gain * one(*cut)
    return gain


def noise(stream_key, extent, width, bound, shards=(), kind=jnp.bfloat16):
    result = width * jax.random.normal(stream_key, extent, jnp.float32)
    if shards:
        result = result * block_scale(stream_key, extent, shards, -0.22, 0.18)
    return jnp.clip(result, -bound, bound).astype(kind)


def setup_inputs(seed: int = 0) -> dict:
    streams_of = jax.random.split(jax.random.key(seed), 8)
    queries = draw_queries(jax.random.fold_in(streams_of[7], 71), 0)
    reply_kv = noise(streams_of[1], (GROUPS, REPLIES, 2, RLEN, KV_HEADS * HD), 1.0, 6.0, ((0, 8), (1, 16), (4, 4)))
    prompt_kv = draw_prompt_kv(jax.random.fold_in(streams_of[7], 71), 0)
    saved_out = noise(streams_of[3], (GROUPS, REPLIES, RLEN, Q_HEADS * HD), 1.0, 6.0, ((0, 8), (1, 16), (3, 4)))
    grad_out = noise(streams_of[4], (GROUPS, REPLIES, RLEN, Q_HEADS * HD), 1.0, 6.0, ((0, 8), (1, 16), (3, 4)))
    prompt_len = draw_prompt_len(jax.random.fold_in(streams_of[7], 71), 0)
    reply_len = draw_reply_len(jax.random.fold_in(streams_of[7], 71), 0)
    return dict(queries=queries, reply_kv=reply_kv, prompt_kv=prompt_kv, saved_out=saved_out, grad_out=grad_out, prompt_len=prompt_len, reply_len=reply_len)


def reference(queries, reply_kv, prompt_kv, saved_out, grad_out, prompt_len, reply_len):
    factor = HD ** -0.5
    positions = jnp.arange(RLEN, dtype=jnp.int32)
    prompt_positions = jnp.arange(PMAX, dtype=jnp.int32)
    causal = positions[None, :] <= positions[:, None]

    def group_pass(group):
        prompt_keys = prompt_kv[group, 0].astype(jnp.float32).reshape(PMAX, KV_HEADS, HD)
        prompt_values = prompt_kv[group, 1].astype(jnp.float32).reshape(PMAX, KV_HEADS, HD)
        visible = jnp.broadcast_to((prompt_positions < prompt_len[group])[None, :], (RLEN, PMAX))
        key_mask = jnp.concatenate([visible, causal], axis=1)

        def member_pass(carry, member):
            key_acc, value_acc, bias_acc = carry
            query = queries[group, member].astype(jnp.float32).reshape(RLEN, KV_HEADS, QPK, HD)
            own_keys = reply_kv[group, member, 0].astype(jnp.float32).reshape(RLEN, KV_HEADS, HD)
            own_values = reply_kv[group, member, 1].astype(jnp.float32).reshape(RLEN, KV_HEADS, HD)
            live = positions < reply_len[group, member]
            out_grad = jnp.where(live[:, None], grad_out[group, member], jnp.zeros((), jnp.bfloat16))
            out_grad = out_grad.astype(jnp.float32).reshape(RLEN, KV_HEADS, QPK, HD)
            saved = saved_out[group, member].astype(jnp.float32).reshape(RLEN, KV_HEADS, QPK, HD)
            key_rows = jnp.concatenate([prompt_keys, own_keys], axis=0)
            value_rows = jnp.concatenate([prompt_values, own_values], axis=0)
            logits = jnp.einsum("thjd,khd->hjtk", query, key_rows) * factor
            logits = jnp.where(key_mask[None, None], logits, -jnp.inf)
            top = jnp.max(logits, axis=-1, keepdims=True)
            log_total = top + jnp.log(jnp.sum(jnp.exp(logits - top), axis=-1, keepdims=True))
            prob = jnp.exp(logits - log_total)
            prob_half = lax.optimization_barrier(prob.astype(jnp.bfloat16)).astype(jnp.float32)
            row_dots = jnp.einsum("thjd,thjd->hjt", out_grad, saved)
            prob_grad = jnp.einsum("thjd,khd->hjtk", out_grad, value_rows)
            score_grad = (prob * (prob_grad - row_dots[..., None])).astype(jnp.bfloat16)
            score_grad = lax.optimization_barrier(score_grad).astype(jnp.float32)
            query_grad = jnp.einsum("hjtk,khd->thjd", score_grad, key_rows) * factor
            query_grad = query_grad.astype(jnp.bfloat16).reshape(RLEN, Q_HEADS * HD)
            key_grad = jnp.einsum("hjtk,thjd->khd", score_grad, query) * factor
            value_grad = jnp.einsum("hjtk,thjd->khd", prob_half, out_grad)
            reply_grad = jnp.stack([key_grad[PMAX:], value_grad[PMAX:]]).reshape(2, RLEN, KV_HEADS * HD)
            carry = (key_acc + key_grad[:PMAX], value_acc + value_grad[:PMAX],
                     bias_acc + jnp.sum(value_grad, axis=0))
            return carry, (query_grad, reply_grad.astype(jnp.bfloat16))

        start = (jnp.zeros((PMAX, KV_HEADS, HD), jnp.float32), jnp.zeros((PMAX, KV_HEADS, HD), jnp.float32),
                 jnp.zeros((KV_HEADS, HD), jnp.float32))
        carry, (query_grads, reply_grads) = lax.scan(member_pass, start, jnp.arange(REPLIES, dtype=jnp.int32))
        prompt_grad = jnp.stack([carry[0], carry[1]]).reshape(2, PMAX, KV_HEADS * HD).astype(jnp.bfloat16)
        return query_grads, reply_grads, prompt_grad, carry[2]

    query_grads, reply_grads, prompt_grads, biases = lax.map(group_pass, jnp.arange(GROUPS, dtype=jnp.int32))
    return query_grads, reply_grads, prompt_grads, jnp.sum(biases, axis=0).reshape(KV_HEADS * HD)
```

```python
import functools
import math

import jax
import jax.numpy as jnp
from jax import lax
from jax.experimental import pallas as pl
from jax.experimental.pallas import tpu as pltpu
from jax.sharding import PartitionSpec as P

NEGATIVE = -1e30
XS = 4
ZS = 4
HD = 128
HEADS = 8
ROWS = 256
SLICE = 64
BLOCK = ZS * SLICE
OWN, LEFT, RIGHT, FAR, REPLY = 0, 1, 2, 3, 4
NT = (((1,), (1,)), ((), ()))
NN = (((1,), (0,)), ((), ()))


def dot(a, b, dims=NN):
    return lax.dot_general(a, b, dims, preferred_element_type=jnp.float32)


def kernel(
    groups,
    plen_ref, rlen_ref, q_hbm, rkv_hbm, pkv_hbm, o_hbm, do_hbm,
    qg_hbm, rg_hbm, pg_hbm, bias_out,
    q_v, do_v, o_v, rkv, kv, probs, dps, dscores, keys_t,
    tops, totals, factors, rowdots, part_k, part_v,
    far_out, far_in, near_out, near_in, col_out, col_in,
    bias_z, bias_x, bias_y, bias_in, qg_v, rg_v, pg_v,
    local_sem, out_sem, z_send, z_recv, x_send, x_recv, relay_send, relay_recv,
    far_send, far_recv, near_send, near_recv, col_send, col_recv,
    bz_send, bz_recv, bx_send, bx_recv, by_send, by_recv,
):
    group = lax.axis_index("grp")
    reply = lax.axis_index("reply")
    x = reply // ZS
    z = reply % ZS
    scale = HD ** (-0.5)
    to_log2 = scale * math.log2(math.e)
    steps = groups.bit_length() - 1

    def at_z(d):
        return {"reply": x * ZS + (z + d) % ZS}

    def at_x(d):
        return {"reply": ((x + d) % XS) * ZS + z}

    def across(i):
        bit = 1 << i
        return {"grp": group + bit - 2 * bit * ((group // bit) % 2)}

    def remote(src, dst, send, recv, device):
        return pltpu.make_async_remote_copy(
            src_ref=src, dst_ref=dst, send_sem=send, recv_sem=recv,
            device_id=device, device_id_type=pl.DeviceIdType.MESH,
        )

    barrier = pltpu.get_barrier_semaphore()
    partners = [at_z(d) for d in range(1, ZS)] + [at_x(d) for d in range(1, XS)]
    partners += [across(i) for i in range(steps)]
    for device in partners:
        pl.semaphore_signal(barrier, inc=1, device_id=device, device_id_type=pl.DeviceIdType.MESH)

    def rows_of(d):
        return pl.ds(pl.multiple_of(((z + d) % ZS) * SLICE, SLICE), SLICE)

    loads = [
        pltpu.make_async_copy(pkv_hbm.at[0], kv.at[x, :, rows_of(0)], local_sem.at[0]),
        pltpu.make_async_copy(do_hbm.at[0, 0], do_v, local_sem.at[1]),
        pltpu.make_async_copy(o_hbm.at[0, 0], o_v, local_sem.at[2]),
        pltpu.make_async_copy(rkv_hbm.at[0, 0], rkv, local_sem.at[3]),
        pltpu.make_async_copy(q_hbm.at[0, 0], q_v, local_sem.at[4]),
    ]
    for load in loads:
        load.start()
    pl.semaphore_wait(barrier, len(partners))

    sends = []

    def start(copy):
        copy.start()
        sends.append(copy)

    def slice_to_neighbours(d, src):
        place = kv.at[x, :, rows_of(-d)]
        for side, way in ((0, 1), (1, -1)):
            start(remote(src, place, x_send.at[side, d], x_recv.at[side, d], at_x(way)))

    for d in range(1, ZS):
        start(remote(pkv_hbm.at[0], kv.at[x, :, rows_of(0)], z_send.at[d], z_recv.at[d], at_z(d)))
    slice_to_neighbours(0, pkv_hbm.at[0])

    def arrived(place, send, recv, device):
        remote(place, place, send, recv, device).wait_recv()

    limit = rlen_ref[0, 0]
    live = lax.broadcasted_iota(jnp.int32, (ROWS, HD), 0) < limit
    ones = jnp.ones((8, HD), jnp.bfloat16)
    loads[1].wait()
    loads[2].wait()
    bias = jnp.zeros((8, HD), jnp.float32)
    for j in range(HEADS):
        cols = slice(j * HD, (j + 1) * HD)
        grad = jnp.where(live, do_v[:, cols].astype(jnp.float32), 0.0)
        do_v[:, cols] = grad.astype(jnp.bfloat16)
        bias = bias + jnp.sum(grad.reshape(ROWS // 8, 8, HD), axis=0)
        product = grad * o_v[:, cols].astype(jnp.float32)
        high = product.astype(jnp.bfloat16)
        low = (product - high.astype(jnp.float32)).astype(jnp.bfloat16)
        rowdots[j] = dot(ones, high, NT) + dot(ones, low, NT)
    bias_z[z] = bias
    for d in range(1, ZS):
        start(remote(bias_z.at[z], bias_z.at[z], bz_send.at[d], bz_recv.at[d], at_z(d)))

    for d in range(1, ZS):
        place = kv.at[x, :, rows_of(-d)]
        arrived(place, z_send.at[d], z_recv.at[d], at_z(d))
        slice_to_neighbours(d, place)

    def first_pass(slot, key, value, visible):
        for j in range(HEADS):
            cols = slice(j * HD, (j + 1) * HD)
            lanes = slice(j * ROWS, (j + 1) * ROWS)
            logits = jnp.where(visible, dot(key, q_v[:, cols], NT) * to_log2, NEGATIVE)
            top = jnp.max(logits, axis=0, keepdims=True)
            power = jnp.exp2(logits - top)
            probs[slot, :, lanes] = power
            tops[slot, j : j + 1, :] = top
            totals[slot, j : j + 1, :] = jnp.sum(power, axis=0, keepdims=True)
            dps[slot, :, lanes] = dot(value, do_v[:, cols], NT) - rowdots[j, 0:1, :]
        columns = slice(slot * BLOCK, (slot + 1) * BLOCK)
        keys_t[:, columns] = key.astype(jnp.float32).T.astype(jnp.bfloat16)

    key_row = lax.broadcasted_iota(jnp.int32, (BLOCK, ROWS), 0)
    prompt_limit = plen_ref[0]

    def prompt_pass(slot, way):
        owner = (x + way) % XS
        first_pass(slot, kv[owner, 0], kv[owner, 1], key_row + owner * BLOCK < prompt_limit)

    loads[3].wait()
    loads[4].wait()
    query_row = lax.broadcasted_iota(jnp.int32, (ROWS, ROWS), 1)
    first_pass(REPLY, rkv[0], rkv[1], key_row <= query_row)

    for d in range(1, ZS):
        there = bias_z.at[(z - d) % ZS]
        arrived(there, bz_send.at[d], bz_recv.at[d], at_z(d))
    bias_x[x] = (bias_z[0] + bias_z[1]) + (bias_z[2] + bias_z[3])
    for d in range(1, XS):
        start(remote(bias_x.at[x], bias_x.at[x], bx_send.at[d], bx_recv.at[d], at_x(d)))

    loads[0].wait()
    prompt_pass(OWN, 0)

    for side, way in ((0, -1), (1, 1)):
        owner = (x + way) % XS
        for d in range(ZS):
            place = kv.at[owner, :, rows_of(-d)]
            arrived(place, x_send.at[side, d], x_recv.at[side, d], at_x(way))
        place = kv.at[owner, side]
        start(remote(place, place, relay_send.at[side], relay_recv.at[side], at_x(-way)))

    for d in range(1, XS):
        there = bias_x.at[(x - d) % XS]
        arrived(there, bx_send.at[d], bx_recv.at[d], at_x(d))
    bias_y[0] = (bias_x[0] + bias_x[1]) + (bias_x[2] + bias_x[3])

    def send_bias(i):
        start(remote(bias_y.at[i], bias_in.at[i], by_send.at[i], by_recv.at[i], across(i)))

    def add_bias(i):
        arrived(bias_in.at[i], by_send.at[i], by_recv.at[i], across(i))
        bias_y[i + 1] = bias_y[i] + bias_in[i]
        if i + 1 < steps:
            send_bias(i + 1)

    if steps > 0:
        send_bias(0)
    prompt_pass(LEFT, -1)
    if steps > 0:
        add_bias(0)
    prompt_pass(RIGHT, 1)
    if steps > 1:
        add_bias(1)
    far = (x + 2) % XS
    for side in (0, 1):
        place = kv.at[far, side]
        arrived(place, relay_send.at[side], relay_recv.at[side], at_x(1))
    prompt_pass(FAR, 2)

    top = jnp.max(tops[...], axis=0)
    total = jnp.zeros((HEADS, ROWS), jnp.float32)
    for slot in range(5):
        total = total + totals[slot] * jnp.exp2(tops[slot] - top)
    for slot in range(5):
        factors[slot] = jnp.exp2(tops[slot] - top) / total

    def second_pass(slot):
        key_part = jnp.zeros((BLOCK, HD), jnp.float32)
        value_part = jnp.zeros((BLOCK, HD), jnp.float32)
        for j in range(HEADS):
            cols = slice(j * HD, (j + 1) * HD)
            lanes = slice(j * ROWS, (j + 1) * ROWS)
            prob = probs[slot, :, lanes] * factors[slot, j : j + 1, :]
            score = (prob * dps[slot, :, lanes]).astype(jnp.bfloat16)
            dscores[slot * BLOCK : (slot + 1) * BLOCK, lanes] = score
            value_part = value_part + dot(prob.astype(jnp.bfloat16), do_v[:, cols])
            key_part = key_part + dot(score, q_v[:, cols])
        return key_part * scale, value_part

    for side, part in enumerate(second_pass(FAR)):
        far_out[side] = part.astype(jnp.bfloat16)
        start(remote(far_out.at[side], far_in.at[side], far_send.at[side], far_recv.at[side],
                     at_x(1 - 2 * side)))
    for side, slot in ((0, RIGHT), (1, LEFT)):
        parts = list(second_pass(slot))
        way = 1 - 2 * side
        arrived(far_in.at[side], far_send.at[side], far_recv.at[side], at_x(way))
        parts[side] = parts[side] + far_in[side].astype(jnp.float32)
        near_out[side, 0] = parts[0].astype(jnp.bfloat16)
        near_out[side, 1] = parts[1].astype(jnp.bfloat16)
        start(remote(near_out.at[side], near_in.at[side], near_send.at[side], near_recv.at[side],
                     at_x(way)))
    part_k[...], part_v[...] = second_pass(OWN)
    if steps > 2:
        add_bias(2)
    bias_out[...] = jnp.sum(bias_y[steps], axis=0, keepdims=True)
    key_part, value_part = second_pass(REPLY)
    rg_v[0] = key_part.astype(jnp.bfloat16)
    rg_v[1] = value_part.astype(jnp.bfloat16)
    reply_store = pltpu.make_async_copy(rg_v, rg_hbm.at[0, 0], out_sem.at[0])
    reply_store.start()

    for side in (0, 1):
        arrived(near_in.at[side], near_send.at[side], near_recv.at[side], at_x(1 - 2 * side))
    for side, part in ((0, part_k), (1, part_v)):
        both = near_in[0, side].astype(jnp.float32) + near_in[1, side].astype(jnp.float32)
        part[...] = part[...] + both
        col_out[side] = part[...].astype(jnp.bfloat16)
    for d in range(1, ZS):
        start(remote(col_out.at[:, rows_of(d)], col_in.at[d], col_send.at[d], col_recv.at[d],
                     at_z(d)))

    for j in range(HEADS):
        cols = slice(j * HD, (j + 1) * HD)
        lanes = slice(j * ROWS, (j + 1) * ROWS)
        turned = dot(keys_t[...], dscores[:, lanes])
        qg_v[:, cols] = (turned.T * scale).astype(jnp.bfloat16)
    query_store = pltpu.make_async_copy(qg_v, qg_hbm.at[0, 0], out_sem.at[1])
    query_store.start()

    for d in range(1, ZS):
        arrived(col_in.at[d], col_send.at[d], col_recv.at[d], at_z(d))
    for side, part in ((0, part_k), (1, part_v)):
        total = part[rows_of(0), :]
        for d in range(1, ZS):
            total = total + col_in[d, side].astype(jnp.float32)
        pg_v[side] = total.astype(jnp.bfloat16)
    prompt_store = pltpu.make_async_copy(pg_v, pg_hbm.at[0], out_sem.at[2])
    prompt_store.start()
    for copy in sends:
        copy.wait_send()
    reply_store.wait()
    query_store.wait()
    prompt_store.wait()


def on_device(groups, queries, reply_kv, prompt_kv, saved_out, grad_out, prompt_len, reply_len):
    half, full = jnp.bfloat16, jnp.float32
    vmem = pltpu.VMEM
    dma = pltpu.SemaphoreType.DMA
    anywhere = pl.BlockSpec(memory_space=pl.ANY)
    smem = pl.BlockSpec(memory_space=pltpu.SMEM)
    steps = groups.bit_length() - 1
    wide = HEADS * HD
    lanes = HEADS * ROWS
    query_grad, reply_grad, prompt_grad, bias = pl.pallas_call(
        functools.partial(kernel, groups),
        out_shape=(
            jax.ShapeDtypeStruct(queries.shape, half),
            jax.ShapeDtypeStruct(reply_kv.shape, half),
            jax.ShapeDtypeStruct(prompt_kv.shape, half),
            jax.ShapeDtypeStruct((1, HD), full),
        ),
        in_specs=[smem, smem] + [anywhere] * 5,
        out_specs=(anywhere, anywhere, anywhere, pl.BlockSpec(memory_space=vmem)),
        scratch_shapes=[
            vmem((ROWS, wide), half),
            vmem((ROWS, wide), half),
            vmem((ROWS, wide), half),
            vmem((2, ROWS, HD), half),
            vmem((XS, 2, BLOCK, HD), half),
            vmem((5, BLOCK, lanes), full),
            vmem((5, BLOCK, lanes), full),
            vmem((5 * BLOCK, lanes), half),
            vmem((HD, 5 * BLOCK), half),
            vmem((5, HEADS, ROWS), full),
            vmem((5, HEADS, ROWS), full),
            vmem((5, HEADS, ROWS), full),
            vmem((HEADS, 8, ROWS), full),
            vmem((BLOCK, HD), full),
            vmem((BLOCK, HD), full),
            vmem((2, BLOCK, HD), half),
            vmem((2, BLOCK, HD), half),
            vmem((2, 2, BLOCK, HD), half),
            vmem((2, 2, BLOCK, HD), half),
            vmem((2, BLOCK, HD), half),
            vmem((ZS, 2, SLICE, HD), half),
            vmem((ZS, 8, HD), full),
            vmem((XS, 8, HD), full),
            vmem((steps + 1, 8, HD), full),
            vmem((max(steps, 1), 8, HD), full),
            vmem((ROWS, wide), half),
            vmem((2, ROWS, HD), half),
            vmem((2, SLICE, HD), half),
            dma((5,)), dma((3,)),
            dma((ZS,)), dma((ZS,)), dma((2, ZS)), dma((2, ZS)), dma((2,)), dma((2,)),
            dma((2,)), dma((2,)), dma((2,)), dma((2,)), dma((ZS,)), dma((ZS,)),
            dma((ZS,)), dma((ZS,)), dma((XS,)), dma((XS,)),
            dma((max(steps, 1),)), dma((max(steps, 1),)),
        ],
        compiler_params=pltpu.CompilerParams(
            collective_id=0, has_side_effects=True, vmem_limit_bytes=56 * 2**20
        ),
        cost_estimate=pl.CostEstimate(
            flops=5 * 2 * lanes * 5 * BLOCK * HD,
            bytes_accessed=5 * 2**20,
            transcendentals=lanes * 5 * BLOCK,
        ),
    )(prompt_len, reply_len, queries, reply_kv, prompt_kv, saved_out, grad_out)
    return query_grad, reply_grad, prompt_grad, bias.reshape(HD)


def solution(mesh):
    in_specs = (
        P("grp", "reply", None, "head"),
        P("grp", "reply", None, None, "head"),
        P("grp", None, "reply", "head"),
        P("grp", "reply", None, "head"),
        P("grp", "reply", None, "head"),
        P("grp"),
        P("grp", "reply"),
    )
    out_specs = (
        P("grp", "reply", None, "head"),
        P("grp", "reply", None, None, "head"),
        P("grp", None, "reply", "head"),
        P("head"),
    )
    return jax.shard_map(
        functools.partial(on_device, mesh.shape["grp"]),
        mesh=mesh, in_specs=in_specs, out_specs=out_specs, check_vma=False,
    )
```

```python
import functools
import math

import jax
import jax.numpy as jnp
from jax import lax
from jax.experimental import pallas as pl
from jax.experimental.pallas import tpu as pltpu
from jax.sharding import PartitionSpec as P

NEGATIVE = -1e30
XS = 4
ZS = 4
HD = 128
HEADS = 8
ROWS = 256
SLICE = 64
BLOCK = ZS * SLICE
NT = (((1,), (1,)), ((), ()))
NN = (((1,), (0,)), ((), ()))


def dot(a, b, dims=NN):
    return lax.dot_general(a, b, dims, preferred_element_type=jnp.float32)


def kernel(
    groups,
    plen_ref, rlen_ref, q_hbm, rkv_hbm, pkv_hbm, o_hbm, do_hbm,
    qg_hbm, rg_hbm, pg_hbm, bias_out,
    q_v, do_v, o_v, kv, mask, probs, dps, dscores, keys_t,
    tops, totals, factors, rowdots, parts,
    far_out, far_in, near_out, near_in, col_out, col_in,
    bias_z, bias_x, bias_y, bias_in, qg_v, rg_v, pg_v,
    local_sem, out_sem, z_send, z_recv, x_send, x_recv, relay_send, relay_recv,
    far_send, far_recv, near_send, near_recv, col_send, col_recv,
    bz_send, bz_recv, bx_send, bx_recv, by_send, by_recv,
):
    group = lax.axis_index("grp")
    reply = lax.axis_index("reply")
    x = reply // ZS
    z = reply % ZS
    scale = HD ** (-0.5)
    to_log2 = scale * math.log2(math.e)
    steps = groups.bit_length() - 1

    def at_z(d):
        return {"reply": x * ZS + (z + d) % ZS}

    def at_x(d):
        return {"reply": ((x + d) % XS) * ZS + z}

    def across(i):
        bit = 1 << i
        return {"grp": group + bit - 2 * bit * ((group // bit) % 2)}

    def remote(src, dst, send, recv, device):
        return pltpu.make_async_remote_copy(
            src_ref=src, dst_ref=dst, send_sem=send, recv_sem=recv,
            device_id=device, device_id_type=pl.DeviceIdType.MESH,
        )

    def arrived(place, send, recv, device):
        remote(place, place, send, recv, device).wait_recv()

    def rows_of(d):
        return pl.ds(pl.multiple_of(((z + d) % ZS) * SLICE, SLICE), SLICE)

    barrier = pltpu.get_barrier_semaphore()
    partners = [at_z(d) for d in range(1, ZS)] + [at_x(d) for d in range(1, XS)]
    partners += [across(i) for i in range(steps)]
    for device in partners:
        pl.semaphore_signal(barrier, inc=1, device_id=device, device_id_type=pl.DeviceIdType.MESH)

    loads = [
        pltpu.make_async_copy(pkv_hbm.at[0], kv.at[x, :, rows_of(0)], local_sem.at[0]),
        pltpu.make_async_copy(do_hbm.at[0, 0], do_v, local_sem.at[1]),
        pltpu.make_async_copy(o_hbm.at[0, 0], o_v, local_sem.at[2]),
        pltpu.make_async_copy(rkv_hbm.at[0, 0], kv.at[XS], local_sem.at[3]),
        pltpu.make_async_copy(q_hbm.at[0, 0], q_v, local_sem.at[4]),
    ]
    for load in loads:
        load.start()
    pl.semaphore_wait(barrier, len(partners))

    own = kv.at[x, :, rows_of(0)]

    def z_copy(d):
        return remote(pkv_hbm.at[0], own, z_send.at[d], z_recv.at[d], at_z(d))

    def x_copy(side, d):
        place = kv.at[x, :, rows_of(-d)]
        src = pkv_hbm.at[0] if d == 0 else place
        return remote(src, place, x_send.at[side, d], x_recv.at[side, d], at_x(1 - 2 * side))

    def relay_copy(side):
        way = 1 - 2 * side
        place = kv.at[(x - way) % XS, side]
        return remote(place, place, relay_send.at[side], relay_recv.at[side], at_x(way))

    def far_copy(side):
        return remote(far_out.at[side], far_in.at[side], far_send.at[side], far_recv.at[side],
                      at_x(1 - 2 * side))

    def near_copy(side):
        return remote(near_out.at[side], near_in.at[side], near_send.at[side], near_recv.at[side],
                      at_x(1 - 2 * side))

    def col_copy(d):
        return remote(col_out.at[:, rows_of(d)], col_in.at[d], col_send.at[d], col_recv.at[d],
                      at_z(d))

    def bz_copy(d):
        return remote(bias_z.at[z], bias_z.at[z], bz_send.at[d], bz_recv.at[d], at_z(d))

    def bx_copy(d):
        return remote(bias_x.at[x], bias_x.at[x], bx_send.at[d], bx_recv.at[d], at_x(d))

    def by_copy(i):
        return remote(bias_y.at[i], bias_in.at[i], by_send.at[i], by_recv.at[i], across(i))

    for d in range(1, ZS):
        z_copy(d).start()
    for side in (0, 1):
        x_copy(side, 0).start()

    for i in (1, 2):
        loads[i].wait()
    limit = rlen_ref[...]
    live = lax.broadcasted_iota(jnp.int32, (ROWS, HD), 0) < limit
    ones = jnp.ones((8, HD), jnp.bfloat16)
    bias = jnp.zeros((8, HD), jnp.float32)
    for j in range(HEADS):
        cols = slice(j * HD, (j + 1) * HD)
        grad = jnp.where(live, do_v[:, cols].astype(jnp.float32), 0.0)
        do_v[:, cols] = grad.astype(jnp.bfloat16)
        bias = bias + jnp.sum(grad.reshape(ROWS // 8, 8, HD), axis=0)
        product = grad * o_v[:, cols].astype(jnp.float32)
        high = product.astype(jnp.bfloat16)
        low = (product - high.astype(jnp.float32)).astype(jnp.bfloat16)
        rowdots[j] = dot(ones, high, NT) + dot(ones, low, NT)
    bias_z[z] = bias
    for d in range(1, ZS):
        bz_copy(d).start()

    for d in range(1, ZS):
        arrived(kv.at[x, :, rows_of(-d)], z_send.at[d], z_recv.at[d], at_z(d))
        for side in (0, 1):
            x_copy(side, d).start()

    for i in (0, 3, 4):
        loads[i].wait()
    prompt_limit = plen_ref[...]
    key_row = lax.broadcasted_iota(jnp.int32, (BLOCK, ROWS), 0)
    query_row = lax.broadcasted_iota(jnp.int32, (BLOCK, ROWS), 1)

    def add_bias(i):
        arrived(bias_in.at[i], by_send.at[i], by_recv.at[i], across(i))
        bias_y[i + 1] = bias_y[i] + bias_in[i]
        if i + 1 < steps:
            by_copy(i + 1).start()

    def first_pass(step, carry):
        @pl.when(step == 1)
        def _():
            for d in range(1, ZS):
                arrived(bias_z.at[(z - d) % ZS], bz_send.at[d], bz_recv.at[d], at_z(d))
            bias_x[x] = (bias_z[0] + bias_z[1]) + (bias_z[2] + bias_z[3])
            for d in range(1, XS):
                bx_copy(d).start()

        @pl.when(step == 2)
        def _():
            for side in (0, 1):
                way = 1 - 2 * side
                for d in range(ZS):
                    arrived(kv.at[(x - way) % XS, :, rows_of(-d)], x_send.at[side, d],
                            x_recv.at[side, d], at_x(way))
                relay_copy(side).start()
            for d in range(1, XS):
                arrived(bias_x.at[(x - d) % XS], bx_send.at[d], bx_recv.at[d], at_x(d))
            bias_y[0] = (bias_x[0] + bias_x[1]) + (bias_x[2] + bias_x[3])
            if steps > 0:
                by_copy(0).start()

        @pl.when(step == 3)
        def _():
            if steps > 0:
                add_bias(0)

        @pl.when(step == 4)
        def _():
            for side in (0, 1):
                arrived(kv.at[(x + 2) % XS, side], relay_send.at[side], relay_recv.at[side],
                        at_x(1 - 2 * side))
            if steps > 1:
                add_bias(1)

        from_reply = 1 - (step + 3) // 4
        turn = step + 3 - 4 * ((step + 3) // 4)
        owner = (x + turn + turn // 2 - 2 * (turn // 3)) % XS
        block = from_reply * XS + (1 - from_reply) * owner
        last = from_reply * query_row + (1 - from_reply) * (prompt_limit - 1 - owner * BLOCK)
        mask[...] = jnp.where(key_row <= last, 0.0, NEGATIVE)
        key, value = kv[block, 0], kv[block, 1]
        columns = pl.ds(pl.multiple_of(step * BLOCK, BLOCK), BLOCK)
        keys_t[:, columns] = key.astype(jnp.float32).T.astype(jnp.bfloat16)
        for j in range(HEADS):
            cols = slice(j * HD, (j + 1) * HD)
            lanes = slice(j * ROWS, (j + 1) * ROWS)
            logits = dot(key, q_v[:, cols], NT) * to_log2 + mask[...]
            top = jnp.max(logits, axis=0, keepdims=True)
            power = jnp.exp2(logits - top)
            probs[step, :, lanes] = power
            tops[step, j : j + 1, :] = top
            totals[step, j : j + 1, :] = jnp.sum(power, axis=0, keepdims=True)
            dps[step, :, lanes] = dot(value, do_v[:, cols], NT) - rowdots[j, 0:1, :]
        return carry

    lax.fori_loop(0, 5, first_pass, 0)

    top = jnp.max(tops[...], axis=0)
    total = jnp.zeros((HEADS, ROWS), jnp.float32)
    for slot in range(5):
        total = total + totals[slot] * jnp.exp2(tops[slot] - top)
    for slot in range(5):
        factors[slot] = jnp.exp2(tops[slot] - top) / total

    def second_pass(turn, carry):
        step = 4 - turn
        key_part = jnp.zeros((BLOCK, HD), jnp.float32)
        value_part = jnp.zeros((BLOCK, HD), jnp.float32)
        rows = pl.ds(pl.multiple_of(step * BLOCK, BLOCK), BLOCK)
        for j in range(HEADS):
            cols = slice(j * HD, (j + 1) * HD)
            lanes = slice(j * ROWS, (j + 1) * ROWS)
            prob = probs[step, :, lanes] * factors[step, j : j + 1, :]
            score = (prob * dps[step, :, lanes]).astype(jnp.bfloat16)
            dscores[rows, lanes] = score
            value_part = value_part + dot(prob.astype(jnp.bfloat16), do_v[:, cols])
            key_part = key_part + dot(score, q_v[:, cols])
        parts[step, 0] = key_part * scale
        parts[step, 1] = value_part

        @pl.when(step == 4)
        def _():
            far_out[...] = parts[4].astype(jnp.bfloat16)
            for side in (0, 1):
                far_copy(side).start()

        for side, slot in ((0, 2), (1, 3)):
            @pl.when(step == slot)
            def _():
                arrived(far_in.at[side], far_send.at[side], far_recv.at[side], at_x(1 - 2 * side))
                other = 1 - side
                both = parts[slot, side] + far_in[side].astype(jnp.float32)
                near_out[side, side] = both.astype(jnp.bfloat16)
                near_out[side, other] = parts[slot, other].astype(jnp.bfloat16)
                near_copy(side).start()

        @pl.when(step == 1)
        def _():
            if steps > 2:
                add_bias(2)

        @pl.when(step == 0)
        def _():
            rg_v[...] = parts[0].astype(jnp.bfloat16)
        return carry

    lax.fori_loop(0, 5, second_pass, 0)
    reply_store = pltpu.make_async_copy(rg_v, rg_hbm.at[0, 0], out_sem.at[0])
    reply_store.start()
    bias_out[...] = jnp.sum(bias_y[steps], axis=0, keepdims=True)

    for side in (0, 1):
        arrived(near_in.at[side], near_send.at[side], near_recv.at[side], at_x(1 - 2 * side))
    parts[1] = parts[1] + (near_in[0].astype(jnp.float32) + near_in[1].astype(jnp.float32))
    col_out[...] = parts[1].astype(jnp.bfloat16)
    for d in range(1, ZS):
        col_copy(d).start()

    for j in range(HEADS):
        cols = slice(j * HD, (j + 1) * HD)
        lanes = slice(j * ROWS, (j + 1) * ROWS)
        turned = dot(keys_t[...], dscores[:, lanes])
        qg_v[:, cols] = (turned.T * scale).astype(jnp.bfloat16)
    query_store = pltpu.make_async_copy(qg_v, qg_hbm.at[0, 0], out_sem.at[1])
    query_store.start()

    for d in range(1, ZS):
        arrived(col_in.at[d], col_send.at[d], col_recv.at[d], at_z(d))
    for side in (0, 1):
        total = parts[1, side, rows_of(0), :]
        for d in range(1, ZS):
            total = total + col_in[d, side].astype(jnp.float32)
        pg_v[side] = total.astype(jnp.bfloat16)
    prompt_store = pltpu.make_async_copy(pg_v, pg_hbm.at[0], out_sem.at[2])
    prompt_store.start()
    started = [z_copy(d) for d in range(1, ZS)] + [col_copy(d) for d in range(1, ZS)]
    started += [x_copy(side, d) for side in (0, 1) for d in range(ZS)]
    started += [f(side) for f in (relay_copy, far_copy, near_copy) for side in (0, 1)]
    started += [bz_copy(d) for d in range(1, ZS)] + [bx_copy(d) for d in range(1, XS)]
    started += [by_copy(i) for i in range(steps)]
    for copy in started:
        copy.wait_send()
    reply_store.wait()
    query_store.wait()
    prompt_store.wait()


def hand_over(*refs):
    sem = refs[-1]
    half = (len(refs) - 1) // 2
    copies = [
        pltpu.make_async_copy(src, dst, sem.at[i])
        for i, (src, dst) in enumerate(zip(refs[:half], refs[half : 2 * half]))
    ]
    for copy in copies:
        copy.start()
    for copy in copies:
        copy.wait()


def on_device(groups, queries, reply_kv, prompt_kv, saved_out, grad_out, prompt_len, reply_len):
    half, full = jnp.bfloat16, jnp.float32
    vmem = pltpu.VMEM
    dma = pltpu.SemaphoreType.DMA
    anywhere = pl.BlockSpec(memory_space=pl.ANY)
    steps = groups.bit_length() - 1
    wide = HEADS * HD
    lanes = HEADS * ROWS
    results = pl.pallas_call(
        functools.partial(kernel, groups),
        out_shape=(
            jax.ShapeDtypeStruct(queries.shape, half),
            jax.ShapeDtypeStruct(reply_kv.shape, half),
            jax.ShapeDtypeStruct(prompt_kv.shape, half),
            jax.ShapeDtypeStruct((1, HD), full),
        ),
        in_specs=[pl.BlockSpec(memory_space=vmem)] * 2 + [anywhere] * 5,
        out_specs=(anywhere, anywhere, anywhere, pl.BlockSpec(memory_space=vmem)),
        scratch_shapes=[
            vmem((ROWS, wide), half),
            vmem((ROWS, wide), half),
            vmem((ROWS, wide), half),
            vmem((XS + 1, 2, BLOCK, HD), half),
            vmem((BLOCK, ROWS), full),
            vmem((5, BLOCK, lanes), full),
            vmem((5, BLOCK, lanes), full),
            vmem((5 * BLOCK, lanes), half),
            vmem((HD, 5 * BLOCK), half),
            vmem((5, HEADS, ROWS), full),
            vmem((5, HEADS, ROWS), full),
            vmem((5, HEADS, ROWS), full),
            vmem((HEADS, 8, ROWS), full),
            vmem((5, 2, BLOCK, HD), full),
            vmem((2, BLOCK, HD), half),
            vmem((2, BLOCK, HD), half),
            vmem((2, 2, BLOCK, HD), half),
            vmem((2, 2, BLOCK, HD), half),
            vmem((2, BLOCK, HD), half),
            vmem((ZS, 2, SLICE, HD), half),
            vmem((ZS, 8, HD), full),
            vmem((XS, 8, HD), full),
            vmem((steps + 1, 8, HD), full),
            vmem((max(steps, 1), 8, HD), full),
            vmem((ROWS, wide), half),
            vmem((2, ROWS, HD), half),
            vmem((2, SLICE, HD), half),
            dma((5,)), dma((3,)),
            dma((ZS,)), dma((ZS,)), dma((2, ZS)), dma((2, ZS)), dma((2,)), dma((2,)),
            dma((2,)), dma((2,)), dma((2,)), dma((2,)), dma((ZS,)), dma((ZS,)),
            dma((ZS,)), dma((ZS,)), dma((XS,)), dma((XS,)),
            dma((max(steps, 1),)), dma((max(steps, 1),)),
        ],
        compiler_params=pltpu.CompilerParams(
            collective_id=0, has_side_effects=True, vmem_limit_bytes=56 * 2**20
        ),
        cost_estimate=pl.CostEstimate(
            flops=5 * 2 * lanes * 5 * BLOCK * HD,
            bytes_accessed=5 * 2**20,
            transcendentals=lanes * 5 * BLOCK,
        ),
    )(prompt_len.reshape(1, 1), reply_len, queries, reply_kv, prompt_kv, saved_out, grad_out)
    query_grad, reply_grad, prompt_grad, bias = pl.pallas_call(
        hand_over,
        out_shape=tuple(jax.ShapeDtypeStruct(r.shape, r.dtype) for r in results),
        in_specs=[anywhere] * 4,
        out_specs=(anywhere,) * 4,
        scratch_shapes=[dma((4,))],
        compiler_params=pltpu.CompilerParams(vmem_limit_bytes=60 * 2**20),
    )(*results)
    return query_grad, reply_grad, prompt_grad, bias.reshape(HD)


def solution(mesh):
    in_specs = (
        P("grp", "reply", None, "head"),
        P("grp", "reply", None, None, "head"),
        P("grp", None, "reply", "head"),
        P("grp", "reply", None, "head"),
        P("grp", "reply", None, "head"),
        P("grp"),
        P("grp", "reply"),
    )
    out_specs = (
        P("grp", "reply", None, "head"),
        P("grp", "reply", None, None, "head"),
        P("grp", None, "reply", "head"),
        P("head"),
    )
    return jax.shard_map(
        functools.partial(on_device, mesh.shape["grp"]),
        mesh=mesh, in_specs=in_specs, out_specs=out_specs, check_vma=False,
    )
```

```python
import functools
import math

import jax
import jax.numpy as jnp
from jax import lax
from jax.experimental import pallas as pl
from jax.experimental.pallas import tpu as pltpu
from jax.sharding import PartitionSpec as P

NEGATIVE = -1e30
XS = 4
ZS = 4
HD = 128
HEADS = 8
ROWS = 256
SLICE = 64
BLOCK = ZS * SLICE
NT = (((1,), (1,)), ((), ()))
NN = (((1,), (0,)), ((), ()))


def dot(a, b, dims=NN):
    return lax.dot_general(a, b, dims, preferred_element_type=jnp.float32)


def kernel(
    groups,
    plen_ref, rlen_ref, q_hbm, rkv_hbm, pkv_hbm, o_hbm, do_hbm,
    qg_hbm, rg_hbm, pg_hbm, bias_out,
    q_v, do_v, o_v, kv, mask, probs, dscores, keys_t,
    tops, totals, factors, rowdots, parts,
    far_out, far_in, near_out, near_in, col_out, col_in,
    bias_z, bias_x, bias_y, bias_in, qg_v, rg_v, pg_v,
    local_sem, out_sem, z_send, z_recv, x_send, x_recv, relay_send, relay_recv,
    far_send, far_recv, near_send, near_recv, col_send, col_recv,
    bz_send, bz_recv, bx_send, bx_recv, by_send, by_recv,
):
    group = lax.axis_index("grp")
    reply = lax.axis_index("reply")
    x = reply // ZS
    z = reply % ZS
    scale = HD ** (-0.5)
    to_log2 = scale * math.log2(math.e)
    steps = groups.bit_length() - 1

    def at_z(d):
        return {"reply": x * ZS + (z + d) % ZS}

    def at_x(d):
        return {"reply": ((x + d) % XS) * ZS + z}

    def across(i):
        bit = 1 << i
        return {"grp": group + bit - 2 * bit * ((group // bit) % 2)}

    def remote(src, dst, send, recv, device):
        return pltpu.make_async_remote_copy(
            src_ref=src, dst_ref=dst, send_sem=send, recv_sem=recv,
            device_id=device, device_id_type=pl.DeviceIdType.MESH,
        )

    def arrived(place, send, recv, device):
        remote(place, place, send, recv, device).wait_recv()

    def rows_of(d):
        return pl.ds(pl.multiple_of(((z + d) % ZS) * SLICE, SLICE), SLICE)

    barrier = pltpu.get_barrier_semaphore()
    partners = [at_z(d) for d in range(1, ZS)] + [at_x(d) for d in range(1, XS)]
    partners += [across(i) for i in range(steps)]
    for device in partners:
        pl.semaphore_signal(barrier, inc=1, device_id=device, device_id_type=pl.DeviceIdType.MESH)

    loads = [
        pltpu.make_async_copy(pkv_hbm.at[0], kv.at[x, :, rows_of(0)], local_sem.at[0]),
        pltpu.make_async_copy(do_hbm.at[0, 0], do_v, local_sem.at[1]),
        pltpu.make_async_copy(o_hbm.at[0, 0], o_v, local_sem.at[2]),
        pltpu.make_async_copy(rkv_hbm.at[0, 0], kv.at[XS], local_sem.at[3]),
        pltpu.make_async_copy(q_hbm.at[0, 0], q_v, local_sem.at[4]),
    ]
    for load in loads:
        load.start()

    def z_copy(kind, d):
        place = kv.at[x, kind, rows_of(0)]
        return remote(place, place, z_send.at[kind, d], z_recv.at[kind, d], at_z(d))

    def z_wait(kind, d):
        arrived(kv.at[x, kind, rows_of(-d)], z_send.at[kind, d], z_recv.at[kind, d], at_z(d))

    def x_copy(kind, side, d):
        place = kv.at[x, kind, rows_of(-d)]
        return remote(place, place, x_send.at[kind, side, d], x_recv.at[kind, side, d],
                      at_x(1 - 2 * side))

    def x_wait(kind, side):
        way = 1 - 2 * side
        for d in range(ZS):
            arrived(kv.at[(x - way) % XS, kind, rows_of(-d)], x_send.at[kind, side, d],
                    x_recv.at[kind, side, d], at_x(way))

    def half_of(side):
        return pl.ds(side * (BLOCK // 2), BLOCK // 2)

    def relay_copy(kind, side):
        way = 1 - 2 * side
        place = kv.at[(x - way) % XS, kind, half_of(side)]
        return remote(place, place, relay_send.at[kind, side], relay_recv.at[kind, side],
                      at_x(way))

    def relay_wait(kind, side):
        arrived(kv.at[(x + 2) % XS, kind, half_of(side)], relay_send.at[kind, side],
                relay_recv.at[kind, side], at_x(1 - 2 * side))

    def far_copy(side):
        return remote(far_out.at[side], far_in.at[side], far_send.at[side], far_recv.at[side],
                      at_x(1 - 2 * side))

    def near_copy(side, d):
        return remote(near_out.at[side, :, rows_of(d)], near_in.at[side, :, rows_of(d)],
                      near_send.at[side, d], near_recv.at[side, d], at_x(1 - 2 * side))

    def near_wait(side, d):
        arrived(near_in.at[side, :, rows_of(d)], near_send.at[side, d], near_recv.at[side, d],
                at_x(1 - 2 * side))

    def col_copy(d):
        return remote(col_out.at[:, rows_of(d)], col_in.at[d], col_send.at[d], col_recv.at[d],
                      at_z(d))

    def bz_copy(d):
        return remote(bias_z.at[z], bias_z.at[z], bz_send.at[d], bz_recv.at[d], at_z(d))

    def bx_copy(d):
        return remote(bias_x.at[x], bias_x.at[x], bx_send.at[d], bx_recv.at[d], at_x(d))

    def by_copy(i):
        return remote(bias_y.at[i], bias_in.at[i], by_send.at[i], by_recv.at[i], across(i))

    loads[0].wait()
    pl.semaphore_wait(barrier, len(partners))
    for kind in (0, 1):
        for d in range(1, ZS):
            z_copy(kind, d).start()
        for side in (0, 1):
            x_copy(kind, side, 0).start()

    for i in (1, 2):
        loads[i].wait()
    limit = rlen_ref[...]
    live = lax.broadcasted_iota(jnp.int32, (ROWS, HD), 0) < limit
    ones = jnp.ones((8, HD), jnp.bfloat16)
    bias = jnp.zeros((8, HD), jnp.float32)
    for j in range(HEADS):
        cols = slice(j * HD, (j + 1) * HD)
        grad = jnp.where(live, do_v[:, cols].astype(jnp.float32), 0.0)
        do_v[:, cols] = grad.astype(jnp.bfloat16)
        bias = bias + jnp.sum(grad.reshape(ROWS // 8, 8, HD), axis=0)
        product = grad * o_v[:, cols].astype(jnp.float32)
        high = product.astype(jnp.bfloat16)
        low = (product - high.astype(jnp.float32)).astype(jnp.bfloat16)
        rowdots[j] = dot(ones, high, NT) + dot(ones, low, NT)
    bias_z[z] = bias
    for d in range(1, ZS):
        bz_copy(d).start()

    def forward(kind):
        for d in range(1, ZS):
            z_wait(kind, d)
            for side in (0, 1):
                x_copy(kind, side, d).start()

    forward(0)
    for i in (3, 4):
        loads[i].wait()
    prompt_limit = plen_ref[...]
    key_row = lax.broadcasted_iota(jnp.int32, (BLOCK, ROWS), 0)
    query_row = lax.broadcasted_iota(jnp.int32, (BLOCK, ROWS), 1)

    def add_bias(i):
        arrived(bias_in.at[i], by_send.at[i], by_recv.at[i], across(i))
        bias_y[i + 1] = bias_y[i] + bias_in[i]
        if i + 1 < steps:
            by_copy(i + 1).start()

    def source(step):
        from_reply = 1 - (step + 3) // 4
        turn = step + 3 - 4 * ((step + 3) // 4)
        owner = (x + turn + turn // 2 - 2 * (turn // 3)) % XS
        return from_reply, owner, from_reply * XS + (1 - from_reply) * owner

    def first_pass(step, carry):
        @pl.when(step == 1)
        def _():
            forward(1)
            for d in range(1, ZS):
                arrived(bias_z.at[(z - d) % ZS], bz_send.at[d], bz_recv.at[d], at_z(d))
            bias_x[x] = (bias_z[0] + bias_z[1]) + (bias_z[2] + bias_z[3])
            for d in range(1, XS):
                bx_copy(d).start()

        @pl.when(step == 2)
        def _():
            for side in (0, 1):
                x_wait(0, side)
                relay_copy(0, side).start()
            for d in range(1, XS):
                arrived(bias_x.at[(x - d) % XS], bx_send.at[d], bx_recv.at[d], at_x(d))
            bias_y[0] = (bias_x[0] + bias_x[1]) + (bias_x[2] + bias_x[3])
            if steps > 0:
                by_copy(0).start()

        @pl.when(step == 3)
        def _():
            for side in (0, 1):
                x_wait(1, side)
                relay_copy(1, side).start()
            if steps > 0:
                add_bias(0)

        @pl.when(step == 4)
        def _():
            for side in (0, 1):
                relay_wait(0, side)
            if steps > 1:
                add_bias(1)

        from_reply, owner, block = source(step)
        last = from_reply * query_row + (1 - from_reply) * (prompt_limit - 1 - owner * BLOCK)
        mask[...] = jnp.where(key_row <= last, 0.0, NEGATIVE)
        key = kv[block, 0]
        columns = pl.ds(pl.multiple_of(step * BLOCK, BLOCK), BLOCK)
        keys_t[:, columns] = key.astype(jnp.float32).T.astype(jnp.bfloat16)
        for j in range(HEADS):
            cols = slice(j * HD, (j + 1) * HD)
            lanes = slice(j * ROWS, (j + 1) * ROWS)
            logits = dot(key, q_v[:, cols], NT) * to_log2 + mask[...]
            top = jnp.max(logits, axis=0, keepdims=True)
            power = jnp.exp2(logits - top)
            probs[step, :, lanes] = power
            tops[step, j : j + 1, :] = top
            totals[step, j : j + 1, :] = jnp.sum(power, axis=0, keepdims=True)
        return carry

    lax.fori_loop(0, 5, first_pass, 0)

    top = jnp.max(tops[...], axis=0)
    total = jnp.zeros((HEADS, ROWS), jnp.float32)
    for slot in range(5):
        total = total + totals[slot] * jnp.exp2(tops[slot] - top)
    for slot in range(5):
        factors[slot] = jnp.exp2(tops[slot] - top) / total

    for side in (0, 1):
        relay_wait(1, side)

    def second_pass(turn, carry):
        step = 4 - turn
        value = kv[source(step)[2], 1]
        key_part = jnp.zeros((BLOCK, HD), jnp.float32)
        value_part = jnp.zeros((BLOCK, HD), jnp.float32)
        rows = pl.ds(pl.multiple_of(step * BLOCK, BLOCK), BLOCK)
        for j in range(HEADS):
            cols = slice(j * HD, (j + 1) * HD)
            lanes = slice(j * ROWS, (j + 1) * ROWS)
            prob = probs[step, :, lanes] * factors[step, j : j + 1, :]
            dprob = dot(value, do_v[:, cols], NT) - rowdots[j, 0:1, :]
            score = (prob * dprob).astype(jnp.bfloat16)
            dscores[rows, lanes] = score
            value_part = value_part + dot(prob.astype(jnp.bfloat16), do_v[:, cols])
            key_part = key_part + dot(score, q_v[:, cols])
        parts[step, 0] = key_part * scale
        parts[step, 1] = value_part

        @pl.when(step == 4)
        def _():
            far_out[...] = parts[4].astype(jnp.bfloat16)
            for side in (0, 1):
                far_copy(side).start()

        for side, slot in ((0, 2), (1, 3)):
            @pl.when(step == slot)
            def _():
                arrived(far_in.at[side], far_send.at[side], far_recv.at[side], at_x(1 - 2 * side))
                other = 1 - side
                both = parts[slot, side] + far_in[side].astype(jnp.float32)
                near_out[side, side] = both.astype(jnp.bfloat16)
                near_out[side, other] = parts[slot, other].astype(jnp.bfloat16)
                for d in (1, 2, 3, 0):
                    near_copy(side, d).start()

        @pl.when(step == 1)
        def _():
            if steps > 2:
                add_bias(2)
            for d in (1, 2, 3, 0):
                for side in (0, 1):
                    near_wait(side, d)
                rows = rows_of(d)
                both = near_in[0, :, rows].astype(jnp.float32) + near_in[1, :, rows].astype(jnp.float32)
                both = parts[1, :, rows] + both
                if d == 0:
                    parts[1, :, rows] = both
                else:
                    col_out[:, rows] = both.astype(jnp.bfloat16)
                    col_copy(d).start()

        @pl.when(step == 0)
        def _():
            rg_v[...] = parts[0].astype(jnp.bfloat16)
        return carry

    lax.fori_loop(0, 5, second_pass, 0)
    reply_store = pltpu.make_async_copy(rg_v, rg_hbm.at[0, 0], out_sem.at[0])
    reply_store.start()
    bias_out[...] = jnp.sum(bias_y[steps], axis=0, keepdims=True)

    for j in range(HEADS):
        cols = slice(j * HD, (j + 1) * HD)
        lanes = slice(j * ROWS, (j + 1) * ROWS)
        turned = dot(keys_t[...], dscores[:, lanes])
        qg_v[:, cols] = (turned.T * scale).astype(jnp.bfloat16)
    query_store = pltpu.make_async_copy(qg_v, qg_hbm.at[0, 0], out_sem.at[1])
    query_store.start()

    for d in range(1, ZS):
        arrived(col_in.at[d], col_send.at[d], col_recv.at[d], at_z(d))
    for side in (0, 1):
        total = parts[1, side, rows_of(0), :]
        for d in range(1, ZS):
            total = total + col_in[d, side].astype(jnp.float32)
        pg_v[side] = total.astype(jnp.bfloat16)
    prompt_store = pltpu.make_async_copy(pg_v, pg_hbm.at[0], out_sem.at[2])
    prompt_store.start()
    started = [z_copy(kind, d) for kind in (0, 1) for d in range(1, ZS)]
    started += [x_copy(kind, side, d) for kind in (0, 1) for side in (0, 1) for d in range(ZS)]
    started += [relay_copy(kind, side) for kind in (0, 1) for side in (0, 1)]
    started += [far_copy(side) for side in (0, 1)] + [col_copy(d) for d in range(1, ZS)]
    started += [near_copy(side, d) for side in (0, 1) for d in range(ZS)]
    started += [bz_copy(d) for d in range(1, ZS)] + [bx_copy(d) for d in range(1, XS)]
    started += [by_copy(i) for i in range(steps)]
    for copy in started:
        copy.wait_send()
    reply_store.wait()
    query_store.wait()
    prompt_store.wait()


def hand_over(*refs):
    half = len(refs) // 2
    for src, dst in zip(refs[:half], refs[half:]):
        dst[...] = src[...]


def on_device(groups, queries, reply_kv, prompt_kv, saved_out, grad_out, prompt_len, reply_len):
    half, full = jnp.bfloat16, jnp.float32
    vmem = pltpu.VMEM
    dma = pltpu.SemaphoreType.DMA
    anywhere = pl.BlockSpec(memory_space=pl.ANY)
    steps = groups.bit_length() - 1
    wide = HEADS * HD
    lanes = HEADS * ROWS
    results = pl.pallas_call(
        functools.partial(kernel, groups),
        out_shape=(
            jax.ShapeDtypeStruct(queries.shape, half),
            jax.ShapeDtypeStruct(reply_kv.shape, half),
            jax.ShapeDtypeStruct(prompt_kv.shape, half),
            jax.ShapeDtypeStruct((1, HD), full),
        ),
        in_specs=[pl.BlockSpec(memory_space=vmem)] * 2 + [anywhere] * 5,
        out_specs=(anywhere, anywhere, anywhere, pl.BlockSpec(memory_space=vmem)),
        scratch_shapes=[
            vmem((ROWS, wide), half),
            vmem((ROWS, wide), half),
            vmem((ROWS, wide), half),
            vmem((XS + 1, 2, BLOCK, HD), half),
            vmem((BLOCK, ROWS), full),
            vmem((5, BLOCK, lanes), full),
            vmem((5 * BLOCK, lanes), half),
            vmem((HD, 5 * BLOCK), half),
            vmem((5, HEADS, ROWS), full),
            vmem((5, HEADS, ROWS), full),
            vmem((5, HEADS, ROWS), full),
            vmem((HEADS, 8, ROWS), full),
            vmem((5, 2, BLOCK, HD), full),
            vmem((2, BLOCK, HD), half),
            vmem((2, BLOCK, HD), half),
            vmem((2, 2, BLOCK, HD), half),
            vmem((2, 2, BLOCK, HD), half),
            vmem((2, BLOCK, HD), half),
            vmem((ZS, 2, SLICE, HD), half),
            vmem((ZS, 8, HD), full),
            vmem((XS, 8, HD), full),
            vmem((steps + 1, 8, HD), full),
            vmem((max(steps, 1), 8, HD), full),
            vmem((ROWS, wide), half),
            vmem((2, ROWS, HD), half),
            vmem((2, SLICE, HD), half),
            dma((5,)), dma((3,)),
            dma((2, ZS)), dma((2, ZS)), dma((2, 2, ZS)), dma((2, 2, ZS)), dma((2, 2)), dma((2, 2)),
            dma((2,)), dma((2,)), dma((2, ZS)), dma((2, ZS)), dma((ZS,)), dma((ZS,)),
            dma((ZS,)), dma((ZS,)), dma((XS,)), dma((XS,)),
            dma((max(steps, 1),)), dma((max(steps, 1),)),
        ],
        compiler_params=pltpu.CompilerParams(
            collective_id=0, has_side_effects=True, vmem_limit_bytes=56 * 2**20
        ),
        cost_estimate=pl.CostEstimate(
            flops=5 * 2 * lanes * 5 * BLOCK * HD,
            bytes_accessed=5 * 2**20,
            transcendentals=lanes * 5 * BLOCK,
        ),
    )(prompt_len.reshape(1, 1), reply_len, queries, reply_kv, prompt_kv, saved_out, grad_out)
    query_grad, reply_grad, prompt_grad, bias = pl.pallas_call(
        hand_over,
        out_shape=tuple(jax.ShapeDtypeStruct(r.shape, r.dtype) for r in results),
        in_specs=[pl.BlockSpec(memory_space=vmem)] * 4,
        out_specs=(pl.BlockSpec(memory_space=vmem),) * 4,
        compiler_params=pltpu.CompilerParams(vmem_limit_bytes=60 * 2**20),
    )(*results)
    return query_grad, reply_grad, prompt_grad, bias.reshape(HD)


def solution(mesh):
    in_specs = (
        P("grp", "reply", None, "head"),
        P("grp", "reply", None, None, "head"),
        P("grp", None, "reply", "head"),
        P("grp", "reply", None, "head"),
        P("grp", "reply", None, "head"),
        P("grp"),
        P("grp", "reply"),
    )
    out_specs = (
        P("grp", "reply", None, "head"),
        P("grp", "reply", None, None, "head"),
        P("grp", None, "reply", "head"),
        P("head"),
    )
    return jax.shard_map(
        functools.partial(on_device, mesh.shape["grp"]),
        mesh=mesh, in_specs=in_specs, out_specs=out_specs, check_vma=False,
    )
```

```python
import functools
import math

import jax
import jax.numpy as jnp
from jax import lax
from jax.experimental import pallas as pl
from jax.experimental.pallas import tpu as pltpu
from jax.sharding import PartitionSpec as P

NEGATIVE = -1e30
XS = 4
ZS = 4
HD = 128
HEADS = 8
ROWS = 256
SLICE = 64
BLOCK = ZS * SLICE
NT = (((1,), (1,)), ((), ()))
NN = (((1,), (0,)), ((), ()))


def dot(a, b, dims=NN):
    return lax.dot_general(a, b, dims, preferred_element_type=jnp.float32)


def kernel(
    groups,
    plen_ref, rlen_ref, q_hbm, rkv_hbm, pkv_hbm, o_hbm, do_hbm,
    qg_hbm, rg_hbm, pg_hbm, bias_out,
    q_v, do_v, o_v, q_st, do_st, q_t, do_t, kv, mask, probs, prob_b, score_b, dscores, keys_t,
    tops, totals, factors, rowdots, parts,
    far_out, far_in, near_out, near_in, col_out, col_in,
    bias_z, bias_x, bias_y, bias_in, qg_v, rg_v, pg_v,
    local_sem, out_sem, z_send, z_recv, x_send, x_recv, relay_send, relay_recv,
    far_send, far_recv, near_send, near_recv, col_send, col_recv,
    bz_send, bz_recv, bx_send, bx_recv, by_send, by_recv,
):
    group = lax.axis_index("grp")
    reply = lax.axis_index("reply")
    x = reply // ZS
    z = reply % ZS
    scale = HD ** (-0.5)
    to_log2 = scale * math.log2(math.e)
    steps = groups.bit_length() - 1

    def at_z(d):
        return {"reply": x * ZS + (z + d) % ZS}

    def at_x(d):
        return {"reply": ((x + d) % XS) * ZS + z}

    def across(i):
        bit = 1 << i
        return {"grp": group + bit - 2 * bit * ((group // bit) % 2)}

    def remote(src, dst, send, recv, device):
        return pltpu.make_async_remote_copy(
            src_ref=src, dst_ref=dst, send_sem=send, recv_sem=recv,
            device_id=device, device_id_type=pl.DeviceIdType.MESH,
        )

    def arrived(place, send, recv, device):
        remote(place, place, send, recv, device).wait_recv()

    def rows_of(d):
        return pl.ds(pl.multiple_of(((z + d) % ZS) * SLICE, SLICE), SLICE)

    barrier = pltpu.get_barrier_semaphore()
    partners = [at_z(d) for d in range(1, ZS)] + [at_x(d) for d in range(1, XS)]
    partners += [across(i) for i in range(steps)]
    for device in partners:
        pl.semaphore_signal(barrier, inc=1, device_id=device, device_id_type=pl.DeviceIdType.MESH)

    loads = [
        pltpu.make_async_copy(pkv_hbm.at[0], kv.at[x, :, rows_of(0)], local_sem.at[0]),
        pltpu.make_async_copy(do_hbm.at[0, 0], do_v, local_sem.at[1]),
        pltpu.make_async_copy(o_hbm.at[0, 0], o_v, local_sem.at[2]),
        pltpu.make_async_copy(rkv_hbm.at[0, 0], kv.at[XS], local_sem.at[3]),
        pltpu.make_async_copy(q_hbm.at[0, 0], q_v, local_sem.at[4]),
    ]
    for load in loads:
        load.start()

    def z_copy(kind, d):
        place = kv.at[x, kind, rows_of(0)]
        return remote(place, place, z_send.at[kind, d], z_recv.at[kind, d], at_z(d))

    def z_wait(kind, d):
        arrived(kv.at[x, kind, rows_of(-d)], z_send.at[kind, d], z_recv.at[kind, d], at_z(d))

    def x_copy(kind, side, d):
        place = kv.at[x, kind, rows_of(-d)]
        return remote(place, place, x_send.at[kind, side, d], x_recv.at[kind, side, d],
                      at_x(1 - 2 * side))

    def x_wait(kind, side):
        way = 1 - 2 * side
        for d in range(ZS):
            arrived(kv.at[(x - way) % XS, kind, rows_of(-d)], x_send.at[kind, side, d],
                    x_recv.at[kind, side, d], at_x(way))

    def half_of(side):
        return pl.ds(side * (BLOCK // 2), BLOCK // 2)

    def relay_copy(kind, side):
        way = 1 - 2 * side
        place = kv.at[(x - way) % XS, kind, half_of(side)]
        return remote(place, place, relay_send.at[kind, side], relay_recv.at[kind, side],
                      at_x(way))

    def relay_wait(kind, side):
        arrived(kv.at[(x + 2) % XS, kind, half_of(side)], relay_send.at[kind, side],
                relay_recv.at[kind, side], at_x(1 - 2 * side))

    def far_copy(side):
        return remote(far_out.at[side], far_in.at[side], far_send.at[side], far_recv.at[side],
                      at_x(1 - 2 * side))

    def near_copy(side, d):
        return remote(near_out.at[side, :, rows_of(d)], near_in.at[side, :, rows_of(d)],
                      near_send.at[side, d], near_recv.at[side, d], at_x(1 - 2 * side))

    def near_wait(side, d):
        arrived(near_in.at[side, :, rows_of(d)], near_send.at[side, d], near_recv.at[side, d],
                at_x(1 - 2 * side))

    def col_copy(d):
        return remote(col_out.at[:, rows_of(d)], col_in.at[d], col_send.at[d], col_recv.at[d],
                      at_z(d))

    def bz_copy(d):
        return remote(bias_z.at[z], bias_z.at[z], bz_send.at[d], bz_recv.at[d], at_z(d))

    def bx_copy(d):
        return remote(bias_x.at[x], bias_x.at[x], bx_send.at[d], bx_recv.at[d], at_x(d))

    def by_copy(i):
        return remote(bias_y.at[i], bias_in.at[i], by_send.at[i], by_recv.at[i], across(i))

    loads[0].wait()
    pl.semaphore_wait(barrier, len(partners))
    for kind in (0, 1):
        for d in range(1, ZS):
            z_copy(kind, d).start()
        for side in (0, 1):
            x_copy(kind, side, 0).start()

    for i in (1, 2):
        loads[i].wait()
    limit = rlen_ref[...]
    live = lax.broadcasted_iota(jnp.int32, (ROWS, HD), 0) < limit
    ones = jnp.ones((8, HD), jnp.bfloat16)
    bias = jnp.zeros((8, HD), jnp.float32)
    for j in range(HEADS):
        cols = slice(j * HD, (j + 1) * HD)
        grad = jnp.where(live, do_v[:, cols].astype(jnp.float32), 0.0)
        do_st[j * ROWS : (j + 1) * ROWS, :] = grad.astype(jnp.bfloat16)
        do_t[j] = grad.T.astype(jnp.bfloat16)
        bias = bias + jnp.sum(grad.reshape(ROWS // 8, 8, HD), axis=0)
        product = grad * o_v[:, cols].astype(jnp.float32)
        high = product.astype(jnp.bfloat16)
        low = (product - high.astype(jnp.float32)).astype(jnp.bfloat16)
        rowdots[j] = dot(ones, high, NT) + dot(ones, low, NT)
    bias_z[z] = bias
    for d in range(1, ZS):
        bz_copy(d).start()

    def forward(kind):
        for d in range(1, ZS):
            z_wait(kind, d)
            for side in (0, 1):
                x_copy(kind, side, d).start()

    forward(0)
    for i in (3, 4):
        loads[i].wait()
    for j in range(HEADS):
        query = q_v[:, j * HD : (j + 1) * HD]
        q_st[j * ROWS : (j + 1) * ROWS, :] = query
        q_t[j] = query.astype(jnp.float32).T.astype(jnp.bfloat16)
    prompt_limit = plen_ref[...]
    key_row = lax.broadcasted_iota(jnp.int32, (BLOCK, ROWS), 0)
    query_row = lax.broadcasted_iota(jnp.int32, (BLOCK, ROWS), 1)

    def add_bias(i):
        arrived(bias_in.at[i], by_send.at[i], by_recv.at[i], across(i))
        bias_y[i + 1] = bias_y[i] + bias_in[i]
        if i + 1 < steps:
            by_copy(i + 1).start()

    def source(step):
        from_reply = 1 - (step + 3) // 4
        turn = step + 3 - 4 * ((step + 3) // 4)
        owner = (x + turn + turn // 2 - 2 * (turn // 3)) % XS
        return from_reply, owner, from_reply * XS + (1 - from_reply) * owner

    def first_pass(step, carry):
        @pl.when(step == 1)
        def _():
            forward(1)
            for d in range(1, ZS):
                arrived(bias_z.at[(z - d) % ZS], bz_send.at[d], bz_recv.at[d], at_z(d))
            bias_x[x] = (bias_z[0] + bias_z[1]) + (bias_z[2] + bias_z[3])
            for d in range(1, XS):
                bx_copy(d).start()

        @pl.when(step == 2)
        def _():
            for side in (0, 1):
                x_wait(0, side)
                relay_copy(0, side).start()
            for d in range(1, XS):
                arrived(bias_x.at[(x - d) % XS], bx_send.at[d], bx_recv.at[d], at_x(d))
            bias_y[0] = (bias_x[0] + bias_x[1]) + (bias_x[2] + bias_x[3])
            if steps > 0:
                by_copy(0).start()

        @pl.when(step == 3)
        def _():
            for side in (0, 1):
                x_wait(1, side)
                relay_copy(1, side).start()
            if steps > 0:
                add_bias(0)

        @pl.when(step == 4)
        def _():
            for side in (0, 1):
                relay_wait(0, side)
            if steps > 1:
                add_bias(1)

        from_reply, owner, block = source(step)
        last = from_reply * query_row + (1 - from_reply) * (prompt_limit - 1 - owner * BLOCK)
        mask[...] = jnp.where(key_row <= last, 0.0, NEGATIVE)
        key = kv[block, 0]
        columns = pl.ds(pl.multiple_of(step * BLOCK, BLOCK), BLOCK)
        keys_t[:, columns] = key.astype(jnp.float32).T.astype(jnp.bfloat16)
        for j in range(HEADS):
            lanes = slice(j * ROWS, (j + 1) * ROWS)
            logits = dot(key, q_t[j]) * to_log2 + mask[...]
            top = jnp.max(logits, axis=0, keepdims=True)
            power = jnp.exp2(logits - top)
            probs[step, :, lanes] = power
            tops[step, j : j + 1, :] = top
            totals[step, j : j + 1, :] = jnp.sum(power, axis=0, keepdims=True)
        return carry

    lax.fori_loop(0, 5, first_pass, 0)

    top = jnp.max(tops[...], axis=0)
    total = jnp.zeros((HEADS, ROWS), jnp.float32)
    for slot in range(5):
        total = total + totals[slot] * jnp.exp2(tops[slot] - top)
    for slot in range(5):
        factors[slot] = jnp.exp2(tops[slot] - top) / total

    for side in (0, 1):
        relay_wait(1, side)

    def second_pass(turn, carry):
        step = 4 - turn
        value = kv[source(step)[2], 1]
        rows = pl.ds(pl.multiple_of(step * BLOCK, BLOCK), BLOCK)
        for j in range(HEADS):
            lanes = slice(j * ROWS, (j + 1) * ROWS)
            prob = probs[step, :, lanes] * factors[step, j : j + 1, :]
            dprob = dot(value, do_t[j]) - rowdots[j, 0:1, :]
            score = (prob * dprob).astype(jnp.bfloat16)
            dscores[rows, lanes] = score
            prob_b[:, lanes] = prob.astype(jnp.bfloat16)
            score_b[:, lanes] = score
        parts[step, 0] = dot(score_b[...], q_st[...]) * scale
        parts[step, 1] = dot(prob_b[...], do_st[...])

        @pl.when(step == 4)
        def _():
            far_out[...] = parts[4].astype(jnp.bfloat16)
            for side in (0, 1):
                far_copy(side).start()

        for side, slot in ((0, 2), (1, 3)):
            @pl.when(step == slot)
            def _():
                arrived(far_in.at[side], far_send.at[side], far_recv.at[side], at_x(1 - 2 * side))
                other = 1 - side
                both = parts[slot, side] + far_in[side].astype(jnp.float32)
                near_out[side, side] = both.astype(jnp.bfloat16)
                near_out[side, other] = parts[slot, other].astype(jnp.bfloat16)
                for d in (1, 2, 3, 0):
                    near_copy(side, d).start()

        @pl.when(step == 1)
        def _():
            if steps > 2:
                add_bias(2)
            for d in (1, 2, 3, 0):
                for side in (0, 1):
                    near_wait(side, d)
                rows = rows_of(d)
                both = near_in[0, :, rows].astype(jnp.float32) + near_in[1, :, rows].astype(jnp.float32)
                both = parts[1, :, rows] + both
                if d == 0:
                    parts[1, :, rows] = both
                else:
                    col_out[:, rows] = both.astype(jnp.bfloat16)
                    col_copy(d).start()

        @pl.when(step == 0)
        def _():
            rg_v[...] = parts[0].astype(jnp.bfloat16)
        return carry

    lax.fori_loop(0, 5, second_pass, 0)
    reply_store = pltpu.make_async_copy(rg_v, rg_hbm.at[0, 0], out_sem.at[0])
    reply_store.start()
    bias_out[...] = jnp.sum(bias_y[steps], axis=0, keepdims=True)

    for j in range(HEADS):
        cols = slice(j * HD, (j + 1) * HD)
        lanes = slice(j * ROWS, (j + 1) * ROWS)
        turned = dot(keys_t[...], dscores[:, lanes])
        qg_v[:, cols] = (turned.T * scale).astype(jnp.bfloat16)
    query_store = pltpu.make_async_copy(qg_v, qg_hbm.at[0, 0], out_sem.at[1])
    query_store.start()

    for d in range(1, ZS):
        arrived(col_in.at[d], col_send.at[d], col_recv.at[d], at_z(d))
    for side in (0, 1):
        total = parts[1, side, rows_of(0), :]
        for d in range(1, ZS):
            total = total + col_in[d, side].astype(jnp.float32)
        pg_v[side] = total.astype(jnp.bfloat16)
    prompt_store = pltpu.make_async_copy(pg_v, pg_hbm.at[0], out_sem.at[2])
    prompt_store.start()
    started = [z_copy(kind, d) for kind in (0, 1) for d in range(1, ZS)]
    started += [x_copy(kind, side, d) for kind in (0, 1) for side in (0, 1) for d in range(ZS)]
    started += [relay_copy(kind, side) for kind in (0, 1) for side in (0, 1)]
    started += [far_copy(side) for side in (0, 1)] + [col_copy(d) for d in range(1, ZS)]
    started += [near_copy(side, d) for side in (0, 1) for d in range(ZS)]
    started += [bz_copy(d) for d in range(1, ZS)] + [bx_copy(d) for d in range(1, XS)]
    started += [by_copy(i) for i in range(steps)]
    for copy in started:
        copy.wait_send()
    reply_store.wait()
    query_store.wait()
    prompt_store.wait()


def hand_over(*refs):
    half = len(refs) // 2
    for src, dst in zip(refs[:half], refs[half:]):
        dst[...] = src[...]


def on_device(groups, queries, reply_kv, prompt_kv, saved_out, grad_out, prompt_len, reply_len):
    half, full = jnp.bfloat16, jnp.float32
    vmem = pltpu.VMEM
    dma = pltpu.SemaphoreType.DMA
    anywhere = pl.BlockSpec(memory_space=pl.ANY)
    steps = groups.bit_length() - 1
    wide = HEADS * HD
    lanes = HEADS * ROWS
    results = pl.pallas_call(
        functools.partial(kernel, groups),
        out_shape=(
            jax.ShapeDtypeStruct(queries.shape, half),
            jax.ShapeDtypeStruct(reply_kv.shape, half),
            jax.ShapeDtypeStruct(prompt_kv.shape, half),
            jax.ShapeDtypeStruct((1, HD), full),
        ),
        in_specs=[pl.BlockSpec(memory_space=vmem)] * 2 + [anywhere] * 5,
        out_specs=(anywhere, anywhere, anywhere, pl.BlockSpec(memory_space=vmem)),
        scratch_shapes=[
            vmem((ROWS, wide), half),
            vmem((ROWS, wide), half),
            vmem((ROWS, wide), half),
            vmem((lanes, HD), half),
            vmem((lanes, HD), half),
            vmem((HEADS, HD, ROWS), half),
            vmem((HEADS, HD, ROWS), half),
            vmem((XS + 1, 2, BLOCK, HD), half),
            vmem((BLOCK, ROWS), full),
            vmem((5, BLOCK, lanes), full),
            vmem((BLOCK, lanes), half),
            vmem((BLOCK, lanes), half),
            vmem((5 * BLOCK, lanes), half),
            vmem((HD, 5 * BLOCK), half),
            vmem((5, HEADS, ROWS), full),
            vmem((5, HEADS, ROWS), full),
            vmem((5, HEADS, ROWS), full),
            vmem((HEADS, 8, ROWS), full),
            vmem((5, 2, BLOCK, HD), full),
            vmem((2, BLOCK, HD), half),
            vmem((2, BLOCK, HD), half),
            vmem((2, 2, BLOCK, HD), half),
            vmem((2, 2, BLOCK, HD), half),
            vmem((2, BLOCK, HD), half),
            vmem((ZS, 2, SLICE, HD), half),
            vmem((ZS, 8, HD), full),
            vmem((XS, 8, HD), full),
            vmem((steps + 1, 8, HD), full),
            vmem((max(steps, 1), 8, HD), full),
            vmem((ROWS, wide), half),
            vmem((2, ROWS, HD), half),
            vmem((2, SLICE, HD), half),
            dma((5,)), dma((3,)),
            dma((2, ZS)), dma((2, ZS)), dma((2, 2, ZS)), dma((2, 2, ZS)), dma((2, 2)), dma((2, 2)),
            dma((2,)), dma((2,)), dma((2, ZS)), dma((2, ZS)), dma((ZS,)), dma((ZS,)),
            dma((ZS,)), dma((ZS,)), dma((XS,)), dma((XS,)),
            dma((max(steps, 1),)), dma((max(steps, 1),)),
        ],
        compiler_params=pltpu.CompilerParams(
            collective_id=0, has_side_effects=True, vmem_limit_bytes=56 * 2**20
        ),
        cost_estimate=pl.CostEstimate(
            flops=5 * 2 * lanes * 5 * BLOCK * HD,
            bytes_accessed=5 * 2**20,
            transcendentals=lanes * 5 * BLOCK,
        ),
    )(prompt_len.reshape(1, 1), reply_len, queries, reply_kv, prompt_kv, saved_out, grad_out)
    query_grad, reply_grad, prompt_grad, bias = pl.pallas_call(
        hand_over,
        out_shape=tuple(jax.ShapeDtypeStruct(r.shape, r.dtype) for r in results),
        in_specs=[pl.BlockSpec(memory_space=vmem)] * 4,
        out_specs=(pl.BlockSpec(memory_space=vmem),) * 4,
        compiler_params=pltpu.CompilerParams(vmem_limit_bytes=60 * 2**20),
    )(*results)
    return query_grad, reply_grad, prompt_grad, bias.reshape(HD)


def solution(mesh):
    in_specs = (
        P("grp", "reply", None, "head"),
        P("grp", "reply", None, None, "head"),
        P("grp", None, "reply", "head"),
        P("grp", "reply", None, "head"),
        P("grp", "reply", None, "head"),
        P("grp"),
        P("grp", "reply"),
    )
    out_specs = (
        P("grp", "reply", None, "head"),
        P("grp", "reply", None, None, "head"),
        P("grp", None, "reply", "head"),
        P("head"),
    )
    return jax.shard_map(
        functools.partial(on_device, mesh.shape["grp"]),
        mesh=mesh, in_specs=in_specs, out_specs=out_specs, check_vma=False,
    )
```

```python
import functools
import math

import jax
import jax.numpy as jnp
from jax import lax
from jax.experimental import pallas as pl
from jax.experimental.pallas import tpu as pltpu
from jax.sharding import PartitionSpec as P

NEGATIVE = -1e30
XS = 4
ZS = 4
HD = 128
HEADS = 8
ROWS = 256
SLICE = 64
BLOCK = ZS * SLICE
NT = (((1,), (1,)), ((), ()))
NN = (((1,), (0,)), ((), ()))


def dot(a, b, dims=NN):
    return lax.dot_general(a, b, dims, preferred_element_type=jnp.float32)


def kernel(
    groups,
    plen_ref, rlen_ref, q_hbm, rkv_hbm, pkv_hbm, o_hbm, do_hbm,
    qg_hbm, rg_hbm, pg_hbm, bias_out,
    q_v, do_v, o_v, q_st, do_st, q_t, do_t, kv, mask, probs, prob_b, score_b, dscores, keys_t,
    tops, totals, factors, rowdots, parts,
    far_out, far_in, near_out, near_in, col_out, col_in,
    bias_z, bias_x, bias_y, qg_v, rg_v, pg_v,
    local_sem, out_sem, z_send, z_recv, x_send, x_recv, relay_send, relay_recv,
    far_send, far_recv, near_send, near_recv, col_send, col_recv,
    bz_send, bz_recv, bx_send, bx_recv, by_send, by_recv,
):
    group = lax.axis_index("grp")
    reply = lax.axis_index("reply")
    x = reply // ZS
    z = reply % ZS
    scale = HD ** (-0.5)
    to_log2 = scale * math.log2(math.e)

    def at_z(d):
        return {"reply": x * ZS + (z + d) % ZS}

    def at_x(d):
        return {"reply": ((x + d) % XS) * ZS + z}

    def at_group(d):
        return {"grp": (group + d) % groups}

    def remote(src, dst, send, recv, device):
        return pltpu.make_async_remote_copy(
            src_ref=src, dst_ref=dst, send_sem=send, recv_sem=recv,
            device_id=device, device_id_type=pl.DeviceIdType.MESH,
        )

    def arrived(place, send, recv, device):
        remote(place, place, send, recv, device).wait_recv()

    def rows_of(d):
        return pl.ds(pl.multiple_of(((z + d) % ZS) * SLICE, SLICE), SLICE)

    barrier = pltpu.get_barrier_semaphore()
    partners = [at_z(d) for d in range(1, ZS)] + [at_x(d) for d in range(1, XS)]
    partners += [at_group(d) for d in range(1, groups)]
    for device in partners:
        pl.semaphore_signal(barrier, inc=1, device_id=device, device_id_type=pl.DeviceIdType.MESH)

    loads = [
        pltpu.make_async_copy(pkv_hbm.at[0], kv.at[x, :, rows_of(0)], local_sem.at[0]),
        pltpu.make_async_copy(do_hbm.at[0, 0], do_v, local_sem.at[1]),
        pltpu.make_async_copy(o_hbm.at[0, 0], o_v, local_sem.at[2]),
        pltpu.make_async_copy(rkv_hbm.at[0, 0], kv.at[XS], local_sem.at[3]),
        pltpu.make_async_copy(q_hbm.at[0, 0], q_v, local_sem.at[4]),
    ]
    for load in loads:
        load.start()

    def z_copy(kind, d):
        place = kv.at[x, kind, rows_of(0)]
        return remote(place, place, z_send.at[kind, d], z_recv.at[kind, d], at_z(d))

    def z_wait(kind, d):
        arrived(kv.at[x, kind, rows_of(-d)], z_send.at[kind, d], z_recv.at[kind, d], at_z(d))

    def x_copy(kind, side, d):
        place = kv.at[x, kind, rows_of(-d)]
        return remote(place, place, x_send.at[kind, side, d], x_recv.at[kind, side, d],
                      at_x(1 - 2 * side))

    def x_wait(kind, side):
        way = 1 - 2 * side
        for d in range(ZS):
            arrived(kv.at[(x - way) % XS, kind, rows_of(-d)], x_send.at[kind, side, d],
                    x_recv.at[kind, side, d], at_x(way))

    def half_of(side):
        return pl.ds(side * (BLOCK // 2), BLOCK // 2)

    def relay_copy(kind, side):
        way = 1 - 2 * side
        place = kv.at[(x - way) % XS, kind, half_of(side)]
        return remote(place, place, relay_send.at[kind, side], relay_recv.at[kind, side],
                      at_x(way))

    def relay_wait(kind, side):
        arrived(kv.at[(x + 2) % XS, kind, half_of(side)], relay_send.at[kind, side],
                relay_recv.at[kind, side], at_x(1 - 2 * side))

    def far_copy(side):
        return remote(far_out.at[side], far_in.at[side], far_send.at[side], far_recv.at[side],
                      at_x(1 - 2 * side))

    def near_copy(side, d):
        return remote(near_out.at[side, :, rows_of(d)], near_in.at[side, :, rows_of(d)],
                      near_send.at[side, d], near_recv.at[side, d], at_x(1 - 2 * side))

    def near_wait(side, d):
        arrived(near_in.at[side, :, rows_of(d)], near_send.at[side, d], near_recv.at[side, d],
                at_x(1 - 2 * side))

    def col_copy(d):
        return remote(col_out.at[:, rows_of(d)], col_in.at[d], col_send.at[d], col_recv.at[d],
                      at_z(d))

    def bz_copy(d):
        return remote(bias_z.at[z], bias_z.at[z], bz_send.at[d], bz_recv.at[d], at_z(d))

    def bx_copy(d):
        return remote(bias_x.at[x], bias_x.at[x], bx_send.at[d], bx_recv.at[d], at_x(d))

    def by_copy(d):
        return remote(bias_y.at[group], bias_y.at[group], by_send.at[d], by_recv.at[d], at_group(d))

    loads[0].wait()
    pl.semaphore_wait(barrier, len(partners))
    for kind in (0, 1):
        for d in range(1, ZS):
            z_copy(kind, d).start()
        for side in (0, 1):
            x_copy(kind, side, 0).start()

    for i in (1, 2):
        loads[i].wait()
    limit = rlen_ref[...]
    live = lax.broadcasted_iota(jnp.int32, (ROWS, HD), 0) < limit
    ones = jnp.ones((8, HD), jnp.bfloat16)
    bias = jnp.zeros((8, HD), jnp.float32)
    for j in range(HEADS):
        cols = slice(j * HD, (j + 1) * HD)
        grad = jnp.where(live, do_v[:, cols].astype(jnp.float32), 0.0)
        do_st[j * ROWS : (j + 1) * ROWS, :] = grad.astype(jnp.bfloat16)
        do_t[j] = grad.T.astype(jnp.bfloat16)
        bias = bias + jnp.sum(grad.reshape(ROWS // 8, 8, HD), axis=0)
        product = grad * o_v[:, cols].astype(jnp.float32)
        high = product.astype(jnp.bfloat16)
        low = (product - high.astype(jnp.float32)).astype(jnp.bfloat16)
        rowdots[j] = dot(ones, high, NT) + dot(ones, low, NT)
    bias_z[z] = bias
    for d in range(1, ZS):
        bz_copy(d).start()

    def forward(kind):
        for d in range(1, ZS):
            z_wait(kind, d)
            for side in (0, 1):
                x_copy(kind, side, d).start()

    for i in (3, 4):
        loads[i].wait()
    for j in range(HEADS):
        query = q_v[:, j * HD : (j + 1) * HD]
        q_st[j * ROWS : (j + 1) * ROWS, :] = query
        q_t[j] = query.astype(jnp.float32).T.astype(jnp.bfloat16)
    prompt_limit = plen_ref[...]
    key_row = lax.broadcasted_iota(jnp.int32, (BLOCK, ROWS), 0)
    query_row = lax.broadcasted_iota(jnp.int32, (BLOCK, ROWS), 1)

    def source(step):
        from_reply = 1 - (step + 3) // 4
        turn = step + 3 - 4 * ((step + 3) // 4)
        owner = (x + turn + turn // 2 - 2 * (turn // 3)) % XS
        return from_reply, owner, from_reply * XS + (1 - from_reply) * owner

    def first_pass(step, carry):
        @pl.when(step == 1)
        def _():
            forward(0)
            forward(1)

        @pl.when(step == 2)
        def _():
            for side in (0, 1):
                x_wait(0, side)
                relay_copy(0, side).start()

        @pl.when(step == 3)
        def _():
            for side in (0, 1):
                x_wait(1, side)
                relay_copy(1, side).start()
            for d in range(1, ZS):
                arrived(bias_z.at[(z - d) % ZS], bz_send.at[d], bz_recv.at[d], at_z(d))
            bias_x[x] = (bias_z[0] + bias_z[1]) + (bias_z[2] + bias_z[3])
            for d in range(1, XS):
                bx_copy(d).start()

        @pl.when(step == 4)
        def _():
            for side in (0, 1):
                relay_wait(0, side)

        from_reply, owner, block = source(step)
        last = from_reply * query_row + (1 - from_reply) * (prompt_limit - 1 - owner * BLOCK)
        mask[...] = jnp.where(key_row <= last, 0.0, NEGATIVE)
        key = kv[block, 0]
        columns = pl.ds(pl.multiple_of(step * BLOCK, BLOCK), BLOCK)
        keys_t[:, columns] = key.astype(jnp.float32).T.astype(jnp.bfloat16)
        for j in range(HEADS):
            lanes = slice(j * ROWS, (j + 1) * ROWS)
            logits = dot(key, q_t[j]) * to_log2 + mask[...]
            top = jnp.max(logits, axis=0, keepdims=True)
            power = jnp.exp2(logits - top)
            probs[step, :, lanes] = power
            tops[step, j : j + 1, :] = top
            totals[step, j : j + 1, :] = jnp.sum(power, axis=0, keepdims=True)
        return carry

    lax.fori_loop(0, 5, first_pass, 0)

    top = jnp.max(tops[...], axis=0)
    total = jnp.zeros((HEADS, ROWS), jnp.float32)
    for slot in range(5):
        total = total + totals[slot] * jnp.exp2(tops[slot] - top)
    for slot in range(5):
        factors[slot] = jnp.exp2(tops[slot] - top) / total

    for side in (0, 1):
        relay_wait(1, side)

    def second_pass(turn, carry):
        step = 4 - turn
        value = kv[source(step)[2], 1]
        rows = pl.ds(pl.multiple_of(step * BLOCK, BLOCK), BLOCK)
        for j in range(HEADS):
            lanes = slice(j * ROWS, (j + 1) * ROWS)
            prob = probs[step, :, lanes] * factors[step, j : j + 1, :]
            dprob = dot(value, do_t[j]) - rowdots[j, 0:1, :]
            score = (prob * dprob).astype(jnp.bfloat16)
            dscores[rows, lanes] = score
            prob_b[:, lanes] = prob.astype(jnp.bfloat16)
            score_b[:, lanes] = score
        parts[step, 0] = dot(score_b[...], q_st[...]) * scale
        parts[step, 1] = dot(prob_b[...], do_st[...])

        @pl.when(step == 4)
        def _():
            far_out[...] = parts[4].astype(jnp.bfloat16)
            for side in (0, 1):
                far_copy(side).start()

        for side, slot in ((0, 2), (1, 3)):
            @pl.when(step == slot)
            def _():
                arrived(far_in.at[side], far_send.at[side], far_recv.at[side], at_x(1 - 2 * side))
                other = 1 - side
                both = parts[slot, side] + far_in[side].astype(jnp.float32)
                near_out[side, side] = both.astype(jnp.bfloat16)
                near_out[side, other] = parts[slot, other].astype(jnp.bfloat16)
                for d in (1, 2, 3, 0):
                    near_copy(side, d).start()
                if slot == 2:
                    for d in range(1, XS):
                        arrived(bias_x.at[(x - d) % XS], bx_send.at[d], bx_recv.at[d], at_x(d))
                    bias_y[group] = (bias_x[0] + bias_x[1]) + (bias_x[2] + bias_x[3])
                    for d in range(1, groups):
                        by_copy(d).start()

        @pl.when(step == 1)
        def _():
            for d in (1, 2, 3, 0):
                for side in (0, 1):
                    near_wait(side, d)
                rows = rows_of(d)
                both = near_in[0, :, rows].astype(jnp.float32) + near_in[1, :, rows].astype(jnp.float32)
                both = parts[1, :, rows] + both
                if d == 0:
                    parts[1, :, rows] = both
                else:
                    col_out[:, rows] = both.astype(jnp.bfloat16)
                    col_copy(d).start()

        @pl.when(step == 0)
        def _():
            rg_v[...] = parts[0].astype(jnp.bfloat16)
        return carry

    lax.fori_loop(0, 5, second_pass, 0)
    reply_store = pltpu.make_async_copy(rg_v, rg_hbm.at[0, 0], out_sem.at[0])
    reply_store.start()
    for j in range(HEADS):
        cols = slice(j * HD, (j + 1) * HD)
        lanes = slice(j * ROWS, (j + 1) * ROWS)
        turned = dot(keys_t[...], dscores[:, lanes])
        qg_v[:, cols] = (turned.T * scale).astype(jnp.bfloat16)
    query_store = pltpu.make_async_copy(qg_v, qg_hbm.at[0, 0], out_sem.at[1])
    query_store.start()

    for d in range(1, ZS):
        arrived(col_in.at[d], col_send.at[d], col_recv.at[d], at_z(d))
    for side in (0, 1):
        total = parts[1, side, rows_of(0), :]
        for d in range(1, ZS):
            total = total + col_in[d, side].astype(jnp.float32)
        pg_v[side] = total.astype(jnp.bfloat16)
    prompt_store = pltpu.make_async_copy(pg_v, pg_hbm.at[0], out_sem.at[2])
    prompt_store.start()
    for d in range(1, groups):
        arrived(bias_y.at[(group - d) % groups], by_send.at[d], by_recv.at[d], at_group(d))
    bias_out[...] = jnp.sum(jnp.sum(bias_y[...], axis=0), axis=0, keepdims=True)
    started = [z_copy(kind, d) for kind in (0, 1) for d in range(1, ZS)]
    started += [x_copy(kind, side, d) for kind in (0, 1) for side in (0, 1) for d in range(ZS)]
    started += [relay_copy(kind, side) for kind in (0, 1) for side in (0, 1)]
    started += [far_copy(side) for side in (0, 1)] + [col_copy(d) for d in range(1, ZS)]
    started += [near_copy(side, d) for side in (0, 1) for d in range(ZS)]
    started += [bz_copy(d) for d in range(1, ZS)] + [bx_copy(d) for d in range(1, XS)]
    started += [by_copy(d) for d in range(1, groups)]
    for copy in started:
        copy.wait_send()
    reply_store.wait()
    query_store.wait()
    prompt_store.wait()


def hand_over(*refs):
    half = len(refs) // 2
    for src, dst in zip(refs[:half], refs[half:]):
        dst[...] = src[...]


def on_device(groups, queries, reply_kv, prompt_kv, saved_out, grad_out, prompt_len, reply_len):
    half, full = jnp.bfloat16, jnp.float32
    vmem = pltpu.VMEM
    dma = pltpu.SemaphoreType.DMA
    anywhere = pl.BlockSpec(memory_space=pl.ANY)
    wide = HEADS * HD
    lanes = HEADS * ROWS
    results = pl.pallas_call(
        functools.partial(kernel, groups),
        out_shape=(
            jax.ShapeDtypeStruct(queries.shape, half),
            jax.ShapeDtypeStruct(reply_kv.shape, half),
            jax.ShapeDtypeStruct(prompt_kv.shape, half),
            jax.ShapeDtypeStruct((1, HD), full),
        ),
        in_specs=[pl.BlockSpec(memory_space=vmem)] * 2 + [anywhere] * 5,
        out_specs=(anywhere, anywhere, anywhere, pl.BlockSpec(memory_space=vmem)),
        scratch_shapes=[
            vmem((ROWS, wide), half),
            vmem((ROWS, wide), half),
            vmem((ROWS, wide), half),
            vmem((lanes, HD), half),
            vmem((lanes, HD), half),
            vmem((HEADS, HD, ROWS), half),
            vmem((HEADS, HD, ROWS), half),
            vmem((XS + 1, 2, BLOCK, HD), half),
            vmem((BLOCK, ROWS), full),
            vmem((5, BLOCK, lanes), full),
            vmem((BLOCK, lanes), half),
            vmem((BLOCK, lanes), half),
            vmem((5 * BLOCK, lanes), half),
            vmem((HD, 5 * BLOCK), half),
            vmem((5, HEADS, ROWS), full),
            vmem((5, HEADS, ROWS), full),
            vmem((5, HEADS, ROWS), full),
            vmem((HEADS, 8, ROWS), full),
            vmem((5, 2, BLOCK, HD), full),
            vmem((2, BLOCK, HD), half),
            vmem((2, BLOCK, HD), half),
            vmem((2, 2, BLOCK, HD), half),
            vmem((2, 2, BLOCK, HD), half),
            vmem((2, BLOCK, HD), half),
            vmem((ZS, 2, SLICE, HD), half),
            vmem((ZS, 8, HD), full),
            vmem((XS, 8, HD), full),
            vmem((groups, 8, HD), full),
            vmem((ROWS, wide), half),
            vmem((2, ROWS, HD), half),
            vmem((2, SLICE, HD), half),
            dma((5,)), dma((3,)),
            dma((2, ZS)), dma((2, ZS)), dma((2, 2, ZS)), dma((2, 2, ZS)), dma((2, 2)), dma((2, 2)),
            dma((2,)), dma((2,)), dma((2, ZS)), dma((2, ZS)), dma((ZS,)), dma((ZS,)),
            dma((ZS,)), dma((ZS,)), dma((XS,)), dma((XS,)),
            dma((groups,)), dma((groups,)),
        ],
        compiler_params=pltpu.CompilerParams(
            collective_id=0, has_side_effects=True, vmem_limit_bytes=56 * 2**20
        ),
        cost_estimate=pl.CostEstimate(
            flops=5 * 2 * lanes * 5 * BLOCK * HD,
            bytes_accessed=5 * 2**20,
            transcendentals=lanes * 5 * BLOCK,
        ),
    )(prompt_len.reshape(1, 1), reply_len, queries, reply_kv, prompt_kv, saved_out, grad_out)
    query_grad, reply_grad, prompt_grad, bias = pl.pallas_call(
        hand_over,
        out_shape=tuple(jax.ShapeDtypeStruct(r.shape, r.dtype) for r in results),
        in_specs=[pl.BlockSpec(memory_space=vmem)] * 4,
        out_specs=(pl.BlockSpec(memory_space=vmem),) * 4,
        compiler_params=pltpu.CompilerParams(vmem_limit_bytes=60 * 2**20),
    )(*results)
    return query_grad, reply_grad, prompt_grad, bias.reshape(HD)


def solution(mesh):
    in_specs = (
        P("grp", "reply", None, "head"),
        P("grp", "reply", None, None, "head"),
        P("grp", None, "reply", "head"),
        P("grp", "reply", None, "head"),
        P("grp", "reply", None, "head"),
        P("grp"),
        P("grp", "reply"),
    )
    out_specs = (
        P("grp", "reply", None, "head"),
        P("grp", "reply", None, None, "head"),
        P("grp", None, "reply", "head"),
        P("head"),
    )
    return jax.shard_map(
        functools.partial(on_device, mesh.shape["grp"]),
        mesh=mesh, in_specs=in_specs, out_specs=out_specs, check_vma=False,
    )
```

```python
import functools
import math

import jax
import jax.numpy as jnp
from jax import lax
from jax.experimental import pallas as pl
from jax.experimental.pallas import tpu as pltpu
from jax.sharding import PartitionSpec as P

NEGATIVE = -1e30
XS = 4
ZS = 4
HD = 128
HEADS = 8
ROWS = 256
SLICE = 64
BLOCK = ZS * SLICE
NT = (((1,), (1,)), ((), ()))
NN = (((1,), (0,)), ((), ()))


def dot(a, b, dims=NN):
    return lax.dot_general(a, b, dims, preferred_element_type=jnp.float32)


def kernel(
    groups,
    plen_ref, rlen_ref, q_hbm, rkv_hbm, pkv_hbm, o_hbm, do_hbm,
    qg_hbm, rg_hbm, pg_hbm, bias_out,
    q_v, do_v, o_v, q_st, do_st, q_t, do_t, kv, mask, probs, dps, prob_b, score_b, dscores, keys_t,
    tops, totals, factors, rowdots, parts,
    near_out, near_in, col_out, col_in,
    bias_z, bias_x, bias_y, qg_v, rg_v, pg_v,
    local_sem, out_sem, z_send, z_recv, x_send, x_recv, relay_send, relay_recv,
    near_send, near_recv, col_send, col_recv,
    bz_send, bz_recv, bx_send, bx_recv, by_send, by_recv,
):
    group = lax.axis_index("grp")
    reply = lax.axis_index("reply")
    x = reply // ZS
    z = reply % ZS
    scale = HD ** (-0.5)
    to_log2 = scale * math.log2(math.e)

    def at_z(d):
        return {"reply": x * ZS + (z + d) % ZS}

    def at_x(d):
        return {"reply": ((x + d) % XS) * ZS + z}

    def at_group(d):
        return {"grp": (group + d) % groups}

    def remote(src, dst, send, recv, device):
        return pltpu.make_async_remote_copy(
            src_ref=src, dst_ref=dst, send_sem=send, recv_sem=recv,
            device_id=device, device_id_type=pl.DeviceIdType.MESH,
        )

    def arrived(place, send, recv, device):
        remote(place, place, send, recv, device).wait_recv()

    def rows_of(d):
        return pl.ds(pl.multiple_of(((z + d) % ZS) * SLICE, SLICE), SLICE)

    barrier = pltpu.get_barrier_semaphore()
    partners = [at_z(d) for d in range(1, ZS)] + [at_x(d) for d in range(1, XS)]
    partners += [at_group(d) for d in range(1, groups)]
    for device in partners:
        pl.semaphore_signal(barrier, inc=1, device_id=device, device_id_type=pl.DeviceIdType.MESH)

    loads = [
        pltpu.make_async_copy(pkv_hbm.at[0], kv.at[x, :, rows_of(0)], local_sem.at[0]),
        pltpu.make_async_copy(do_hbm.at[0, 0], do_v, local_sem.at[1]),
        pltpu.make_async_copy(o_hbm.at[0, 0], o_v, local_sem.at[2]),
        pltpu.make_async_copy(rkv_hbm.at[0, 0], kv.at[XS], local_sem.at[3]),
        pltpu.make_async_copy(q_hbm.at[0, 0], q_v, local_sem.at[4]),
    ]
    for load in loads:
        load.start()

    def z_copy(kind, d):
        place = kv.at[x, kind, rows_of(0)]
        return remote(place, place, z_send.at[kind, d], z_recv.at[kind, d], at_z(d))

    def z_wait(kind, d):
        arrived(kv.at[x, kind, rows_of(-d)], z_send.at[kind, d], z_recv.at[kind, d], at_z(d))

    def x_copy(kind, way, d):
        place = kv.at[x, kind, rows_of(-d)]
        return remote(place, place, x_send.at[kind, way, d], x_recv.at[kind, way, d], at_x(way))

    def x_wait(kind, way):
        for d in range(ZS):
            arrived(kv.at[(x - way) % XS, kind, rows_of(-d)], x_send.at[kind, way, d],
                    x_recv.at[kind, way, d], at_x(way))

    x_ways = ((1, 3, 2), (1, 3))

    def half_of(side):
        return pl.ds(side * (BLOCK // 2), BLOCK // 2)

    def relay_copy(side):
        way = 1 - 2 * side
        place = kv.at[(x - way) % XS, 1, half_of(side)]
        return remote(place, place, relay_send.at[side], relay_recv.at[side], at_x(way))

    def relay_wait(side):
        arrived(kv.at[(x + 2) % XS, 1, half_of(side)], relay_send.at[side],
                relay_recv.at[side], at_x(1 - 2 * side))

    def near_copy(way, d):
        return remote(near_out.at[way, :, rows_of(d)], near_in.at[way, :, rows_of(d)],
                      near_send.at[way, d], near_recv.at[way, d], at_x(way))

    def near_wait(way, d):
        arrived(near_in.at[way, :, rows_of(d)], near_send.at[way, d], near_recv.at[way, d],
                at_x(way))

    def col_copy(d):
        return remote(col_out.at[:, rows_of(d)], col_in.at[d], col_send.at[d], col_recv.at[d],
                      at_z(d))

    def bz_copy(d):
        return remote(bias_z.at[z], bias_z.at[z], bz_send.at[d], bz_recv.at[d], at_z(d))

    def bx_copy(d):
        return remote(bias_x.at[x], bias_x.at[x], bx_send.at[d], bx_recv.at[d], at_x(d))

    def by_copy(d):
        return remote(bias_y.at[group], bias_y.at[group], by_send.at[d], by_recv.at[d], at_group(d))

    loads[0].wait()
    pl.semaphore_wait(barrier, len(partners))
    for kind in (0, 1):
        for d in range(1, ZS):
            z_copy(kind, d).start()
        for way in x_ways[kind]:
            x_copy(kind, way, 0).start()

    for i in (1, 2):
        loads[i].wait()
    limit = rlen_ref[...]
    live = lax.broadcasted_iota(jnp.int32, (ROWS, HD), 0) < limit
    ones = jnp.ones((8, HD), jnp.bfloat16)
    bias = jnp.zeros((8, HD), jnp.float32)
    for j in range(HEADS):
        cols = slice(j * HD, (j + 1) * HD)
        grad = jnp.where(live, do_v[:, cols].astype(jnp.float32), 0.0)
        do_st[j * ROWS : (j + 1) * ROWS, :] = grad.astype(jnp.bfloat16)
        do_t[j] = grad.T.astype(jnp.bfloat16)
        bias = bias + jnp.sum(grad.reshape(ROWS // 8, 8, HD), axis=0)
        product = grad * o_v[:, cols].astype(jnp.float32)
        high = product.astype(jnp.bfloat16)
        low = (product - high.astype(jnp.float32)).astype(jnp.bfloat16)
        rowdots[j] = dot(ones, high, NT) + dot(ones, low, NT)
    bias_z[z] = bias
    for d in range(1, ZS):
        bz_copy(d).start()

    def forward(kind):
        for d in range(1, ZS):
            z_wait(kind, d)
            for way in x_ways[kind]:
                x_copy(kind, way, d).start()

    for i in (3, 4):
        loads[i].wait()
    for j in range(HEADS):
        query = q_v[:, j * HD : (j + 1) * HD]
        q_st[j * ROWS : (j + 1) * ROWS, :] = query
        q_t[j] = query.astype(jnp.float32).T.astype(jnp.bfloat16)
    prompt_limit = plen_ref[...]
    key_row = lax.broadcasted_iota(jnp.int32, (BLOCK, ROWS), 0)
    query_row = lax.broadcasted_iota(jnp.int32, (BLOCK, ROWS), 1)

    def source(step):
        from_reply = 1 - (step + 3) // 4
        turn = step + 3 - 4 * ((step + 3) // 4)
        owner = (x + turn + turn // 2 - 2 * (turn // 3)) % XS
        return from_reply, owner, from_reply * XS + (1 - from_reply) * owner

    def value_grads(step):
        value = kv[source(step)[2], 1]
        for j in range(HEADS):
            lanes = slice(j * ROWS, (j + 1) * ROWS)
            dps[step, :, lanes] = dot(value, do_t[j]) - rowdots[j, 0:1, :]

    def first_pass(step, carry):
        @pl.when(step == 1)
        def _():
            forward(0)
            forward(1)

        @pl.when(step == 3)
        def _():
            for side in (0, 1):
                x_wait(1, 1 + 2 * side)
                relay_copy(side).start()
            for d in range(1, ZS):
                arrived(bias_z.at[(z - d) % ZS], bz_send.at[d], bz_recv.at[d], at_z(d))
            bias_x[x] = (bias_z[0] + bias_z[1]) + (bias_z[2] + bias_z[3])
            for d in range(1, XS):
                bx_copy(d).start()

        @pl.when(step > 0)
        def _():
            value_grads(step - 1)

        for slot, way in ((2, 3), (3, 1), (4, 2)):
            @pl.when(step == slot)
            def _():
                x_wait(0, way)

        from_reply, owner, block = source(step)
        last = from_reply * query_row + (1 - from_reply) * (prompt_limit - 1 - owner * BLOCK)
        mask[...] = jnp.where(key_row <= last, 0.0, NEGATIVE)
        key = kv[block, 0]
        columns = pl.ds(pl.multiple_of(step * BLOCK, BLOCK), BLOCK)
        keys_t[:, columns] = key.astype(jnp.float32).T.astype(jnp.bfloat16)
        for j in range(HEADS):
            lanes = slice(j * ROWS, (j + 1) * ROWS)
            logits = dot(key, q_t[j]) * to_log2 + mask[...]
            top = jnp.max(logits, axis=0, keepdims=True)
            power = jnp.exp2(logits - top)
            probs[step, :, lanes] = power
            tops[step, j : j + 1, :] = top
            totals[step, j : j + 1, :] = jnp.sum(power, axis=0, keepdims=True)
        return carry

    lax.fori_loop(0, 5, first_pass, 0)

    top = jnp.max(tops[...], axis=0)
    total = jnp.zeros((HEADS, ROWS), jnp.float32)
    for slot in range(5):
        total = total + totals[slot] * jnp.exp2(tops[slot] - top)
    for slot in range(5):
        factors[slot] = jnp.exp2(tops[slot] - top) / total

    for side in (0, 1):
        relay_wait(side)
    value_grads(4)

    def second_pass(turn, carry):
        step = 4 - turn
        rows = pl.ds(pl.multiple_of(step * BLOCK, BLOCK), BLOCK)
        for j in range(HEADS):
            lanes = slice(j * ROWS, (j + 1) * ROWS)
            prob = probs[step, :, lanes] * factors[step, j : j + 1, :]
            score = (prob * dps[step, :, lanes]).astype(jnp.bfloat16)
            dscores[rows, lanes] = score
            prob_b[:, lanes] = prob.astype(jnp.bfloat16)
            score_b[:, lanes] = score
        parts[step, 0] = dot(score_b[...], q_st[...]) * scale
        parts[step, 1] = dot(prob_b[...], do_st[...])

        for slot, way in ((4, 2), (3, 3), (2, 1)):
            @pl.when(step == slot)
            def _():
                near_out[way] = parts[slot].astype(jnp.bfloat16)
                for d in (1, 2, 3, 0):
                    near_copy(way, d).start()
                if slot == 2:
                    for d in range(1, XS):
                        arrived(bias_x.at[(x - d) % XS], bx_send.at[d], bx_recv.at[d], at_x(d))
                    bias_y[group] = (bias_x[0] + bias_x[1]) + (bias_x[2] + bias_x[3])
                    for d in range(1, groups):
                        by_copy(d).start()

        @pl.when(step == 1)
        def _():
            for d in (1, 2, 3, 0):
                rows = rows_of(d)
                total = parts[1, :, rows]
                for way in (2, 3, 1):
                    near_wait(way, d)
                    total = total + near_in[way, :, rows].astype(jnp.float32)
                if d == 0:
                    parts[1, :, rows] = total
                else:
                    col_out[:, rows] = total.astype(jnp.bfloat16)
                    col_copy(d).start()

        @pl.when(step == 0)
        def _():
            rg_v[...] = parts[0].astype(jnp.bfloat16)
        return carry

    lax.fori_loop(0, 5, second_pass, 0)
    reply_store = pltpu.make_async_copy(rg_v, rg_hbm.at[0, 0], out_sem.at[0])
    reply_store.start()
    for j in range(HEADS):
        cols = slice(j * HD, (j + 1) * HD)
        lanes = slice(j * ROWS, (j + 1) * ROWS)
        turned = dot(keys_t[...], dscores[:, lanes])
        qg_v[:, cols] = (turned.T * scale).astype(jnp.bfloat16)
    query_store = pltpu.make_async_copy(qg_v, qg_hbm.at[0, 0], out_sem.at[1])
    query_store.start()

    for d in range(1, ZS):
        arrived(col_in.at[d], col_send.at[d], col_recv.at[d], at_z(d))
    for side in (0, 1):
        total = parts[1, side, rows_of(0), :]
        for d in range(1, ZS):
            total = total + col_in[d, side].astype(jnp.float32)
        pg_v[side] = total.astype(jnp.bfloat16)
    prompt_store = pltpu.make_async_copy(pg_v, pg_hbm.at[0], out_sem.at[2])
    prompt_store.start()
    for d in range(1, groups):
        arrived(bias_y.at[(group - d) % groups], by_send.at[d], by_recv.at[d], at_group(d))
    bias_out[...] = jnp.sum(jnp.sum(bias_y[...], axis=0), axis=0, keepdims=True)
    started = [z_copy(kind, d) for kind in (0, 1) for d in range(1, ZS)]
    started += [x_copy(kind, way, d) for kind in (0, 1) for way in x_ways[kind] for d in range(ZS)]
    started += [relay_copy(side) for side in (0, 1)] + [col_copy(d) for d in range(1, ZS)]
    started += [near_copy(way, d) for way in range(1, XS) for d in range(ZS)]
    started += [bz_copy(d) for d in range(1, ZS)] + [bx_copy(d) for d in range(1, XS)]
    started += [by_copy(d) for d in range(1, groups)]
    for copy in started:
        copy.wait_send()
    reply_store.wait()
    query_store.wait()
    prompt_store.wait()


def hand_over(
    query_in, reply_in, prompt_in, bias_in, query_out, reply_out, prompt_out, bias_out,
    query_v, reply_v, prompt_v, bias_v, in_sem, out_sem,
):
    piece = ROWS // 4
    moves = [
        (query_in.at[0, 0, rows], query_v.at[rows], query_out.at[0, 0, rows])
        for rows in (pl.ds(i * piece, piece) for i in range(4))
    ]
    moves += [(reply_in, reply_v, reply_out), (prompt_in, prompt_v, prompt_out)]
    moves += [(bias_in, bias_v, bias_out)]
    enter = [pltpu.make_async_copy(m[0], m[1], in_sem.at[i]) for i, m in enumerate(moves)]
    leave = [pltpu.make_async_copy(m[1], m[2], out_sem.at[i]) for i, m in enumerate(moves)]
    for copy in enter:
        copy.start()
    for before, after in zip(enter, leave):
        before.wait()
        after.start()
    for copy in leave:
        copy.wait()


def on_device(groups, queries, reply_kv, prompt_kv, saved_out, grad_out, prompt_len, reply_len):
    half, full = jnp.bfloat16, jnp.float32
    vmem = pltpu.VMEM
    dma = pltpu.SemaphoreType.DMA
    anywhere = pl.BlockSpec(memory_space=pl.ANY)
    wide = HEADS * HD
    lanes = HEADS * ROWS
    results = pl.pallas_call(
        functools.partial(kernel, groups),
        out_shape=(
            jax.ShapeDtypeStruct(queries.shape, half),
            jax.ShapeDtypeStruct(reply_kv.shape, half),
            jax.ShapeDtypeStruct(prompt_kv.shape, half),
            jax.ShapeDtypeStruct((1, HD), full),
        ),
        in_specs=[pl.BlockSpec(memory_space=vmem)] * 2 + [anywhere] * 5,
        out_specs=(anywhere, anywhere, anywhere, pl.BlockSpec(memory_space=vmem)),
        scratch_shapes=[
            vmem((ROWS, wide), half),
            vmem((ROWS, wide), half),
            vmem((ROWS, wide), half),
            vmem((lanes, HD), half),
            vmem((lanes, HD), half),
            vmem((HEADS, HD, ROWS), half),
            vmem((HEADS, HD, ROWS), half),
            vmem((XS + 1, 2, BLOCK, HD), half),
            vmem((BLOCK, ROWS), full),
            vmem((5, BLOCK, lanes), full),
            vmem((5, BLOCK, lanes), full),
            vmem((BLOCK, lanes), half),
            vmem((BLOCK, lanes), half),
            vmem((5 * BLOCK, lanes), half),
            vmem((HD, 5 * BLOCK), half),
            vmem((5, HEADS, ROWS), full),
            vmem((5, HEADS, ROWS), full),
            vmem((5, HEADS, ROWS), full),
            vmem((HEADS, 8, ROWS), full),
            vmem((5, 2, BLOCK, HD), full),
            vmem((XS, 2, BLOCK, HD), half),
            vmem((XS, 2, BLOCK, HD), half),
            vmem((2, BLOCK, HD), half),
            vmem((ZS, 2, SLICE, HD), half),
            vmem((ZS, 8, HD), full),
            vmem((XS, 8, HD), full),
            vmem((groups, 8, HD), full),
            vmem((ROWS, wide), half),
            vmem((2, ROWS, HD), half),
            vmem((2, SLICE, HD), half),
            dma((5,)), dma((3,)),
            dma((2, ZS)), dma((2, ZS)), dma((2, XS, ZS)), dma((2, XS, ZS)), dma((2,)), dma((2,)),
            dma((XS, ZS)), dma((XS, ZS)), dma((ZS,)), dma((ZS,)),
            dma((ZS,)), dma((ZS,)), dma((XS,)), dma((XS,)),
            dma((groups,)), dma((groups,)),
        ],
        compiler_params=pltpu.CompilerParams(
            collective_id=0, has_side_effects=True, vmem_limit_bytes=56 * 2**20
        ),
        cost_estimate=pl.CostEstimate(
            flops=5 * 2 * lanes * 5 * BLOCK * HD,
            bytes_accessed=5 * 2**20,
            transcendentals=lanes * 5 * BLOCK,
        ),
    )(prompt_len.reshape(1, 1), reply_len, queries, reply_kv, prompt_kv, saved_out, grad_out)
    query_grad, reply_grad, prompt_grad, bias = pl.pallas_call(
        hand_over,
        out_shape=tuple(jax.ShapeDtypeStruct(r.shape, r.dtype) for r in results),
        in_specs=[anywhere] * 4,
        out_specs=(anywhere,) * 4,
        scratch_shapes=[
            vmem((ROWS, wide), half),
            vmem(reply_kv.shape, half),
            vmem(prompt_kv.shape, half),
            vmem((1, HD), full),
            dma((7,)),
            dma((7,)),
        ],
        compiler_params=pltpu.CompilerParams(vmem_limit_bytes=60 * 2**20),
    )(*results)
    return query_grad, reply_grad, prompt_grad, bias.reshape(HD)


def solution(mesh):
    in_specs = (
        P("grp", "reply", None, "head"),
        P("grp", "reply", None, None, "head"),
        P("grp", None, "reply", "head"),
        P("grp", "reply", None, "head"),
        P("grp", "reply", None, "head"),
        P("grp"),
        P("grp", "reply"),
    )
    out_specs = (
        P("grp", "reply", None, "head"),
        P("grp", "reply", None, None, "head"),
        P("grp", None, "reply", "head"),
        P("head"),
    )
    return jax.shard_map(
        functools.partial(on_device, mesh.shape["grp"]),
        mesh=mesh, in_specs=in_specs, out_specs=out_specs, check_vma=False,
    )
```

```python
import functools
import math

import jax
import jax.numpy as jnp
from jax import lax
from jax.experimental import pallas as pl
from jax.experimental.pallas import tpu as pltpu
from jax.sharding import PartitionSpec as P

NEGATIVE = -1e30
XS = 4
ZS = 4
HD = 128
HEADS = 8
ROWS = 256
SLICE = 64
BLOCK = ZS * SLICE
NT = (((1,), (1,)), ((), ()))
NN = (((1,), (0,)), ((), ()))


def dot(a, b, dims=NN):
    return lax.dot_general(a, b, dims, preferred_element_type=jnp.float32)


def kernel(
    groups,
    plen_ref, rlen_ref, q_hbm, rkv_hbm, pkv_hbm, o_hbm, do_hbm,
    qg_hbm, rg_hbm, pg_hbm, bias_out,
    q_v, do_v, o_v, q_st, do_st, q_t, do_t, kv, mask, probs, dps, prob_b, score_b, dscores, keys_t,
    tops, totals, factors, rowdots, parts,
    near_out, near_in, col_out, col_in, last_in,
    bias_z, bias_x, bias_y, qg_v, rg_v, pg_v,
    local_sem, out_sem, key_send, key_recv, z_send, z_recv, x_send, x_recv, relay_send, relay_recv,
    near_send, near_recv, col_send, col_recv, last_send, last_recv,
    bz_send, bz_recv, bx_send, bx_recv, by_send, by_recv,
):
    group = lax.axis_index("grp")
    reply = lax.axis_index("reply")
    x = reply // ZS
    z = reply % ZS
    scale = HD ** (-0.5)
    to_log2 = scale * math.log2(math.e)

    def at(way, d):
        return {"reply": ((x + way) % XS) * ZS + (z + d) % ZS}

    def at_z(d):
        return {"reply": x * ZS + (z + d) % ZS}

    def at_x(d):
        return {"reply": ((x + d) % XS) * ZS + z}

    def at_group(d):
        return {"grp": (group + d) % groups}

    def remote(src, dst, send, recv, device):
        return pltpu.make_async_remote_copy(
            src_ref=src, dst_ref=dst, send_sem=send, recv_sem=recv,
            device_id=device, device_id_type=pl.DeviceIdType.MESH,
        )

    def arrived(place, send, recv, device):
        remote(place, place, send, recv, device).wait_recv()

    def rows_of(d):
        return pl.ds(pl.multiple_of(((z + d) % ZS) * SLICE, SLICE), SLICE)

    barrier = pltpu.get_barrier_semaphore()
    partners = [at(way, d) for way in range(XS) for d in range(ZS) if way + d > 0]
    partners += [at_group(d) for d in range(1, groups)]
    for device in partners:
        pl.semaphore_signal(barrier, inc=1, device_id=device, device_id_type=pl.DeviceIdType.MESH)

    loads = [
        pltpu.make_async_copy(pkv_hbm.at[0], kv.at[x, :, rows_of(0)], local_sem.at[0]),
        pltpu.make_async_copy(do_hbm.at[0, 0], do_v, local_sem.at[1]),
        pltpu.make_async_copy(o_hbm.at[0, 0], o_v, local_sem.at[2]),
        pltpu.make_async_copy(rkv_hbm.at[0, 0], kv.at[XS], local_sem.at[3]),
        pltpu.make_async_copy(q_hbm.at[0, 0], q_v, local_sem.at[4]),
    ]
    for load in loads:
        load.start()

    def key_copy(way, d):
        place = kv.at[x, 0, rows_of(0)]
        return remote(place, place, key_send.at[way, d], key_recv.at[way, d], at(way, d))

    def key_wait(way):
        for d in range(ZS):
            if way + d > 0:
                arrived(kv.at[(x - way) % XS, 0, rows_of(-d)], key_send.at[way, d],
                        key_recv.at[way, d], at(way, d))

    def z_copy(d):
        place = kv.at[x, 1, rows_of(0)]
        return remote(place, place, z_send.at[d], z_recv.at[d], at_z(d))

    def x_copy(way, d):
        place = kv.at[x, 1, rows_of(-d)]
        return remote(place, place, x_send.at[way, d], x_recv.at[way, d], at_x(way))

    def x_wait(way):
        for d in range(ZS):
            arrived(kv.at[(x - way) % XS, 1, rows_of(-d)], x_send.at[way, d], x_recv.at[way, d],
                    at_x(way))

    def half_of(side):
        return pl.ds(side * (BLOCK // 2), BLOCK // 2)

    def relay_copy(side):
        way = 1 - 2 * side
        place = kv.at[(x - way) % XS, 1, half_of(side)]
        return remote(place, place, relay_send.at[side], relay_recv.at[side], at_x(way))

    def relay_wait(side):
        arrived(kv.at[(x + 2) % XS, 1, half_of(side)], relay_send.at[side],
                relay_recv.at[side], at_x(1 - 2 * side))

    def near_copy(way, d):
        return remote(near_out.at[way, :, rows_of(d)], near_in.at[way, :, rows_of(d)],
                      near_send.at[way, d], near_recv.at[way, d], at_x(way))

    def near_wait(way, d):
        arrived(near_in.at[way, :, rows_of(d)], near_send.at[way, d], near_recv.at[way, d],
                at_x(way))

    def last_copy(d):
        return remote(near_out.at[1, :, rows_of(d)], last_in.at[d], last_send.at[d],
                      last_recv.at[d], at(1, d))

    def last_wait(d):
        arrived(last_in.at[d], last_send.at[d], last_recv.at[d], at(1, d))

    def col_copy(d):
        return remote(col_out.at[:, rows_of(d)], col_in.at[d], col_send.at[d], col_recv.at[d],
                      at_z(d))

    def bz_copy(d):
        return remote(bias_z.at[z], bias_z.at[z], bz_send.at[d], bz_recv.at[d], at_z(d))

    def bx_copy(d):
        return remote(bias_x.at[x], bias_x.at[x], bx_send.at[d], bx_recv.at[d], at_x(d))

    def by_copy(d):
        return remote(bias_y.at[group], bias_y.at[group], by_send.at[d], by_recv.at[d], at_group(d))

    loads[0].wait()
    pl.semaphore_wait(barrier, len(partners))
    for way in (0, 3, 1, 2):
        for d in range(ZS):
            if way + d > 0:
                key_copy(way, d).start()
    for d in range(1, ZS):
        z_copy(d).start()
    for way in (1, 3):
        x_copy(way, 0).start()

    for i in (1, 2):
        loads[i].wait()
    limit = rlen_ref[...]
    live = lax.broadcasted_iota(jnp.int32, (ROWS, HD), 0) < limit
    ones = jnp.ones((8, HD), jnp.bfloat16)
    bias = jnp.zeros((8, HD), jnp.float32)
    for j in range(HEADS):
        cols = slice(j * HD, (j + 1) * HD)
        grad = jnp.where(live, do_v[:, cols].astype(jnp.float32), 0.0)
        do_st[j * ROWS : (j + 1) * ROWS, :] = grad.astype(jnp.bfloat16)
        do_t[j] = grad.T.astype(jnp.bfloat16)
        bias = bias + jnp.sum(grad.reshape(ROWS // 8, 8, HD), axis=0)
        product = grad * o_v[:, cols].astype(jnp.float32)
        high = product.astype(jnp.bfloat16)
        low = (product - high.astype(jnp.float32)).astype(jnp.bfloat16)
        rowdots[j] = dot(ones, high, NT) + dot(ones, low, NT)
    bias_z[z] = bias
    for d in range(1, ZS):
        bz_copy(d).start()

    for i in (3, 4):
        loads[i].wait()
    for j in range(HEADS):
        query = q_v[:, j * HD : (j + 1) * HD]
        q_st[j * ROWS : (j + 1) * ROWS, :] = query
        q_t[j] = query.astype(jnp.float32).T.astype(jnp.bfloat16)
    prompt_limit = plen_ref[...]
    key_row = lax.broadcasted_iota(jnp.int32, (BLOCK, ROWS), 0)
    query_row = lax.broadcasted_iota(jnp.int32, (BLOCK, ROWS), 1)

    def source(step):
        from_reply = 1 - (step + 3) // 4
        turn = step + 3 - 4 * ((step + 3) // 4)
        owner = (x + turn + turn // 2 - 2 * (turn // 3)) % XS
        return from_reply, owner, from_reply * XS + (1 - from_reply) * owner

    def value_grads(step):
        value = kv[source(step)[2], 1]
        for j in range(HEADS):
            lanes = slice(j * ROWS, (j + 1) * ROWS)
            dps[step, :, lanes] = dot(value, do_t[j]) - rowdots[j, 0:1, :]

    def first_pass(step, carry):
        @pl.when(step == 1)
        def _():
            for d in range(1, ZS):
                arrived(kv.at[x, 1, rows_of(-d)], z_send.at[d], z_recv.at[d], at_z(d))
                for way in (1, 3):
                    x_copy(way, d).start()
            key_wait(0)

        @pl.when(step == 3)
        def _():
            for side in (0, 1):
                x_wait(1 + 2 * side)
                relay_copy(side).start()
            for d in range(1, ZS):
                arrived(bias_z.at[(z - d) % ZS], bz_send.at[d], bz_recv.at[d], at_z(d))
            bias_x[x] = (bias_z[0] + bias_z[1]) + (bias_z[2] + bias_z[3])
            for d in range(1, XS):
                bx_copy(d).start()

        @pl.when(step > 0)
        def _():
            value_grads(step - 1)

        for slot, way in ((2, 3), (3, 1), (4, 2)):
            @pl.when(step == slot)
            def _():
                key_wait(way)

        from_reply, owner, block = source(step)
        last = from_reply * query_row + (1 - from_reply) * (prompt_limit - 1 - owner * BLOCK)
        mask[...] = jnp.where(key_row <= last, 0.0, NEGATIVE)
        key = kv[block, 0]
        columns = pl.ds(pl.multiple_of(step * BLOCK, BLOCK), BLOCK)
        keys_t[:, columns] = key.astype(jnp.float32).T.astype(jnp.bfloat16)
        for j in range(HEADS):
            lanes = slice(j * ROWS, (j + 1) * ROWS)
            logits = dot(key, q_t[j]) * to_log2 + mask[...]
            top = jnp.max(logits, axis=0, keepdims=True)
            power = jnp.exp2(logits - top)
            probs[step, :, lanes] = power
            tops[step, j : j + 1, :] = top
            totals[step, j : j + 1, :] = jnp.sum(power, axis=0, keepdims=True)
        return carry

    lax.fori_loop(0, 5, first_pass, 0)

    top = jnp.max(tops[...], axis=0)
    total = jnp.zeros((HEADS, ROWS), jnp.float32)
    for slot in range(5):
        total = total + totals[slot] * jnp.exp2(tops[slot] - top)
    for slot in range(5):
        factors[slot] = jnp.exp2(tops[slot] - top) / total

    for side in (0, 1):
        relay_wait(side)
    value_grads(4)

    def second_pass(turn, carry):
        step = 4 - turn
        rows = pl.ds(pl.multiple_of(step * BLOCK, BLOCK), BLOCK)
        for j in range(HEADS):
            lanes = slice(j * ROWS, (j + 1) * ROWS)
            prob = probs[step, :, lanes] * factors[step, j : j + 1, :]
            score = (prob * dps[step, :, lanes]).astype(jnp.bfloat16)
            dscores[rows, lanes] = score
            prob_b[:, lanes] = prob.astype(jnp.bfloat16)
            score_b[:, lanes] = score
        parts[step, 0] = dot(score_b[...], q_st[...]) * scale
        parts[step, 1] = dot(prob_b[...], do_st[...])

        for slot, way in ((4, 2), (3, 3), (2, 1)):
            @pl.when(step == slot)
            def _():
                near_out[way] = parts[slot].astype(jnp.bfloat16)
                for d in (1, 2, 3, 0):
                    (last_copy(d) if slot == 2 else near_copy(way, d)).start()
                if slot == 2:
                    for d in range(1, XS):
                        arrived(bias_x.at[(x - d) % XS], bx_send.at[d], bx_recv.at[d], at_x(d))
                    bias_y[group] = (bias_x[0] + bias_x[1]) + (bias_x[2] + bias_x[3])
                    for d in range(1, groups):
                        by_copy(d).start()

        @pl.when(step == 1)
        def _():
            for d in (1, 2, 3, 0):
                rows = rows_of(d)
                total = parts[1, :, rows]
                for way in (2, 3):
                    near_wait(way, d)
                    total = total + near_in[way, :, rows].astype(jnp.float32)
                if d == 0:
                    parts[1, :, rows] = total
                else:
                    col_out[:, rows] = total.astype(jnp.bfloat16)
                    col_copy(d).start()

        @pl.when(step == 0)
        def _():
            rg_v[...] = parts[0].astype(jnp.bfloat16)
        return carry

    lax.fori_loop(0, 5, second_pass, 0)
    reply_store = pltpu.make_async_copy(rg_v, rg_hbm.at[0, 0], out_sem.at[0])
    reply_store.start()
    for j in range(HEADS):
        cols = slice(j * HD, (j + 1) * HD)
        lanes = slice(j * ROWS, (j + 1) * ROWS)
        turned = dot(keys_t[...], dscores[:, lanes])
        qg_v[:, cols] = (turned.T * scale).astype(jnp.bfloat16)
    query_store = pltpu.make_async_copy(qg_v, qg_hbm.at[0, 0], out_sem.at[1])
    query_store.start()

    for d in range(1, ZS):
        arrived(col_in.at[d], col_send.at[d], col_recv.at[d], at_z(d))
    for d in range(ZS):
        last_wait(d)
    for side in (0, 1):
        total = parts[1, side, rows_of(0), :]
        for d in range(1, ZS):
            total = total + col_in[d, side].astype(jnp.float32)
        for d in range(ZS):
            total = total + last_in[d, side].astype(jnp.float32)
        pg_v[side] = total.astype(jnp.bfloat16)
    prompt_store = pltpu.make_async_copy(pg_v, pg_hbm.at[0], out_sem.at[2])
    prompt_store.start()
    for d in range(1, groups):
        arrived(bias_y.at[(group - d) % groups], by_send.at[d], by_recv.at[d], at_group(d))
    bias_out[...] = jnp.sum(jnp.sum(bias_y[...], axis=0), axis=0, keepdims=True)
    started = [key_copy(way, d) for way in range(XS) for d in range(ZS) if way + d > 0]
    started += [z_copy(d) for d in range(1, ZS)]
    started += [x_copy(way, d) for way in (1, 3) for d in range(ZS)]
    started += [relay_copy(side) for side in (0, 1)] + [col_copy(d) for d in range(1, ZS)]
    started += [near_copy(way, d) for way in (2, 3) for d in range(ZS)]
    started += [last_copy(d) for d in range(ZS)]
    started += [bz_copy(d) for d in range(1, ZS)] + [bx_copy(d) for d in range(1, XS)]
    started += [by_copy(d) for d in range(1, groups)]
    for copy in started:
        copy.wait_send()
    reply_store.wait()
    query_store.wait()
    prompt_store.wait()


def hand_over(
    query_in, reply_in, prompt_in, bias_in, query_out, reply_out, prompt_out, bias_out,
    query_v, reply_v, prompt_v, bias_v, in_sem, out_sem,
):
    piece = ROWS // 4
    moves = [
        (query_in.at[0, 0, rows], query_v.at[rows], query_out.at[0, 0, rows])
        for rows in (pl.ds(i * piece, piece) for i in range(4))
    ]
    moves += [(reply_in, reply_v, reply_out), (prompt_in, prompt_v, prompt_out)]
    moves += [(bias_in, bias_v, bias_out)]
    enter = [pltpu.make_async_copy(m[0], m[1], in_sem.at[i]) for i, m in enumerate(moves)]
    leave = [pltpu.make_async_copy(m[1], m[2], out_sem.at[i]) for i, m in enumerate(moves)]
    for copy in enter:
        copy.start()
    for before, after in zip(enter, leave):
        before.wait()
        after.start()
    for copy in leave:
        copy.wait()


def on_device(groups, queries, reply_kv, prompt_kv, saved_out, grad_out, prompt_len, reply_len):
    half, full = jnp.bfloat16, jnp.float32
    vmem = pltpu.VMEM
    dma = pltpu.SemaphoreType.DMA
    anywhere = pl.BlockSpec(memory_space=pl.ANY)
    wide = HEADS * HD
    lanes = HEADS * ROWS
    results = pl.pallas_call(
        functools.partial(kernel, groups),
        out_shape=(
            jax.ShapeDtypeStruct(queries.shape, half),
            jax.ShapeDtypeStruct(reply_kv.shape, half),
            jax.ShapeDtypeStruct(prompt_kv.shape, half),
            jax.ShapeDtypeStruct((1, HD), full),
        ),
        in_specs=[pl.BlockSpec(memory_space=vmem)] * 2 + [anywhere] * 5,
        out_specs=(anywhere, anywhere, anywhere, pl.BlockSpec(memory_space=vmem)),
        scratch_shapes=[
            vmem((ROWS, wide), half),
            vmem((ROWS, wide), half),
            vmem((ROWS, wide), half),
            vmem((lanes, HD), half),
            vmem((lanes, HD), half),
            vmem((HEADS, HD, ROWS), half),
            vmem((HEADS, HD, ROWS), half),
            vmem((XS + 1, 2, BLOCK, HD), half),
            vmem((BLOCK, ROWS), full),
            vmem((5, BLOCK, lanes), full),
            vmem((5, BLOCK, lanes), full),
            vmem((BLOCK, lanes), half),
            vmem((BLOCK, lanes), half),
            vmem((5 * BLOCK, lanes), half),
            vmem((HD, 5 * BLOCK), half),
            vmem((5, HEADS, ROWS), full),
            vmem((5, HEADS, ROWS), full),
            vmem((5, HEADS, ROWS), full),
            vmem((HEADS, 8, ROWS), full),
            vmem((5, 2, BLOCK, HD), full),
            vmem((XS, 2, BLOCK, HD), half),
            vmem((XS, 2, BLOCK, HD), half),
            vmem((2, BLOCK, HD), half),
            vmem((ZS, 2, SLICE, HD), half),
            vmem((ZS, 2, SLICE, HD), half),
            vmem((ZS, 8, HD), full),
            vmem((XS, 8, HD), full),
            vmem((groups, 8, HD), full),
            vmem((ROWS, wide), half),
            vmem((2, ROWS, HD), half),
            vmem((2, SLICE, HD), half),
            dma((5,)), dma((3,)),
            dma((XS, ZS)), dma((XS, ZS)),
            dma((ZS,)), dma((ZS,)), dma((XS, ZS)), dma((XS, ZS)), dma((2,)), dma((2,)),
            dma((XS, ZS)), dma((XS, ZS)), dma((ZS,)), dma((ZS,)), dma((ZS,)), dma((ZS,)),
            dma((ZS,)), dma((ZS,)), dma((XS,)), dma((XS,)),
            dma((groups,)), dma((groups,)),
        ],
        compiler_params=pltpu.CompilerParams(
            collective_id=0, has_side_effects=True, vmem_limit_bytes=56 * 2**20
        ),
        cost_estimate=pl.CostEstimate(
            flops=5 * 2 * lanes * 5 * BLOCK * HD,
            bytes_accessed=5 * 2**20,
            transcendentals=lanes * 5 * BLOCK,
        ),
    )(prompt_len.reshape(1, 1), reply_len, queries, reply_kv, prompt_kv, saved_out, grad_out)
    query_grad, reply_grad, prompt_grad, bias = pl.pallas_call(
        hand_over,
        out_shape=tuple(jax.ShapeDtypeStruct(r.shape, r.dtype) for r in results),
        in_specs=[anywhere] * 4,
        out_specs=(anywhere,) * 4,
        scratch_shapes=[
            vmem((ROWS, wide), half),
            vmem(reply_kv.shape, half),
            vmem(prompt_kv.shape, half),
            vmem((1, HD), full),
            dma((7,)),
            dma((7,)),
        ],
        compiler_params=pltpu.CompilerParams(vmem_limit_bytes=60 * 2**20),
    )(*results)
    return query_grad, reply_grad, prompt_grad, bias.reshape(HD)


def solution(mesh):
    in_specs = (
        P("grp", "reply", None, "head"),
        P("grp", "reply", None, None, "head"),
        P("grp", None, "reply", "head"),
        P("grp", "reply", None, "head"),
        P("grp", "reply", None, "head"),
        P("grp"),
        P("grp", "reply"),
    )
    out_specs = (
        P("grp", "reply", None, "head"),
        P("grp", "reply", None, None, "head"),
        P("grp", None, "reply", "head"),
        P("head"),
    )
    return jax.shard_map(
        functools.partial(on_device, mesh.shape["grp"]),
        mesh=mesh, in_specs=in_specs, out_specs=out_specs, check_vma=False,
    )
```

```python
import functools
import math

import jax
import jax.numpy as jnp
from jax import lax
from jax.experimental import pallas as pl
from jax.experimental.pallas import tpu as pltpu
from jax.sharding import PartitionSpec as P

NEGATIVE = -1e30
XS = 4
ZS = 4
HD = 128
HEADS = 8
ROWS = 256
SLICE = 64
BLOCK = ZS * SLICE
NT = (((1,), (1,)), ((), ()))
NN = (((1,), (0,)), ((), ()))


def dot(a, b, dims=NN):
    return lax.dot_general(a, b, dims, preferred_element_type=jnp.float32)


def kernel(
    groups,
    plen_ref, rlen_ref, q_hbm, rkv_hbm, pkv_hbm, o_hbm, do_hbm,
    qg_hbm, rg_hbm, pg_hbm, bias_out,
    q_v, do_v, o_v, q_st, do_st, q_t, do_t, kv, mask, probs, dps, prob_b, score_b, dscores, keys_t,
    tops, totals, factors, rowdots, parts,
    near_out, near_in, col_out, col_in,
    bias_z, bias_x, bias_y, qg_v, rg_v, pg_v,
    local_sem, out_sem, z_send, z_recv, x_send, x_recv, relay_send, relay_recv,
    near_send, near_recv, col_send, col_recv,
    bz_send, bz_recv, bx_send, bx_recv, by_send, by_recv,
):
    group = lax.axis_index("grp")
    reply = lax.axis_index("reply")
    x = reply // ZS
    z = reply % ZS
    scale = HD ** (-0.5)
    to_log2 = scale * math.log2(math.e)

    def at_z(d):
        return {"reply": x * ZS + (z + d) % ZS}

    def at_x(d):
        return {"reply": ((x + d) % XS) * ZS + z}

    def at_group(d):
        return {"grp": (group + d) % groups}

    def remote(src, dst, send, recv, device):
        return pltpu.make_async_remote_copy(
            src_ref=src, dst_ref=dst, send_sem=send, recv_sem=recv,
            device_id=device, device_id_type=pl.DeviceIdType.MESH,
        )

    def arrived(place, send, recv, device):
        remote(place, place, send, recv, device).wait_recv()

    def rows_of(d):
        return pl.ds(pl.multiple_of(((z + d) % ZS) * SLICE, SLICE), SLICE)

    barrier = pltpu.get_barrier_semaphore()
    partners = [at_z(d) for d in range(1, ZS)] + [at_x(d) for d in range(1, XS)]
    partners += [at_group(d) for d in range(1, groups)]
    for device in partners:
        pl.semaphore_signal(barrier, inc=1, device_id=device, device_id_type=pl.DeviceIdType.MESH)

    loads = [
        pltpu.make_async_copy(pkv_hbm.at[0], kv.at[x, :, rows_of(0)], local_sem.at[0]),
        pltpu.make_async_copy(do_hbm.at[0, 0], do_v, local_sem.at[1]),
        pltpu.make_async_copy(o_hbm.at[0, 0], o_v, local_sem.at[2]),
        pltpu.make_async_copy(rkv_hbm.at[0, 0], kv.at[XS], local_sem.at[3]),
        pltpu.make_async_copy(q_hbm.at[0, 0], q_v, local_sem.at[4]),
    ]
    for load in loads:
        load.start()

    def z_copy(kind, d):
        place = kv.at[x, kind, rows_of(0)]
        return remote(place, place, z_send.at[kind, d], z_recv.at[kind, d], at_z(d))

    def z_wait(kind, d):
        arrived(kv.at[x, kind, rows_of(-d)], z_send.at[kind, d], z_recv.at[kind, d], at_z(d))

    def x_copy(kind, way, d):
        place = kv.at[x, kind, rows_of(-d)]
        return remote(place, place, x_send.at[kind, way, d], x_recv.at[kind, way, d], at_x(way))

    def x_wait(kind, way):
        for d in range(ZS):
            arrived(kv.at[(x - way) % XS, kind, rows_of(-d)], x_send.at[kind, way, d],
                    x_recv.at[kind, way, d], at_x(way))

    x_ways = ((1, 3), (1, 3))

    def half_of(side):
        return pl.ds(side * (BLOCK // 2), BLOCK // 2)

    def relay_copy(kind, side):
        way = 1 - 2 * side
        place = kv.at[(x - way) % XS, kind, half_of(side)]
        return remote(place, place, relay_send.at[kind, side], relay_recv.at[kind, side],
                      at_x(way))

    def relay_wait(kind, side):
        arrived(kv.at[(x + 2) % XS, kind, half_of(side)], relay_send.at[kind, side],
                relay_recv.at[kind, side], at_x(1 - 2 * side))

    def near_copy(way, d):
        return remote(near_out.at[way, :, rows_of(d)], near_in.at[way, :, rows_of(d)],
                      near_send.at[way, d], near_recv.at[way, d], at_x(way))

    def near_wait(way, d):
        arrived(near_in.at[way, :, rows_of(d)], near_send.at[way, d], near_recv.at[way, d],
                at_x(way))

    def col_copy(d):
        return remote(col_out.at[:, rows_of(d)], col_in.at[d], col_send.at[d], col_recv.at[d],
                      at_z(d))

    def bz_copy(d):
        return remote(bias_z.at[z], bias_z.at[z], bz_send.at[d], bz_recv.at[d], at_z(d))

    def bx_copy(d):
        return remote(bias_x.at[x], bias_x.at[x], bx_send.at[d], bx_recv.at[d], at_x(d))

    def by_copy(d):
        return remote(bias_y.at[group], bias_y.at[group], by_send.at[d], by_recv.at[d], at_group(d))

    loads[0].wait()
    pl.semaphore_wait(barrier, len(partners))
    for kind in (0, 1):
        for d in range(1, ZS):
            z_copy(kind, d).start()
        for way in x_ways[kind]:
            x_copy(kind, way, 0).start()

    for i in (1, 2):
        loads[i].wait()
    limit = rlen_ref[...]
    live = lax.broadcasted_iota(jnp.int32, (ROWS, HD), 0) < limit
    ones = jnp.ones((8, HD), jnp.bfloat16)
    bias = jnp.zeros((8, HD), jnp.float32)
    for j in range(HEADS):
        cols = slice(j * HD, (j + 1) * HD)
        grad = jnp.where(live, do_v[:, cols].astype(jnp.float32), 0.0)
        do_st[j * ROWS : (j + 1) * ROWS, :] = grad.astype(jnp.bfloat16)
        do_t[j] = grad.T.astype(jnp.bfloat16)
        bias = bias + jnp.sum(grad.reshape(ROWS // 8, 8, HD), axis=0)
        product = grad * o_v[:, cols].astype(jnp.float32)
        high = product.astype(jnp.bfloat16)
        low = (product - high.astype(jnp.float32)).astype(jnp.bfloat16)
        rowdots[j] = dot(ones, high, NT) + dot(ones, low, NT)
    bias_z[z] = bias
    for d in range(1, ZS):
        bz_copy(d).start()

    def forward(kind):
        for d in range(1, ZS):
            z_wait(kind, d)
            for way in x_ways[kind]:
                x_copy(kind, way, d).start()

    for i in (3, 4):
        loads[i].wait()
    for j in range(HEADS):
        query = q_v[:, j * HD : (j + 1) * HD]
        q_st[j * ROWS : (j + 1) * ROWS, :] = query
        q_t[j] = query.astype(jnp.float32).T.astype(jnp.bfloat16)
    prompt_limit = plen_ref[...]
    key_row = lax.broadcasted_iota(jnp.int32, (BLOCK, ROWS), 0)
    query_row = lax.broadcasted_iota(jnp.int32, (BLOCK, ROWS), 1)

    def source(step):
        from_reply = 1 - (step + 3) // 4
        turn = step + 3 - 4 * ((step + 3) // 4)
        owner = (x + turn + turn // 2 - 2 * (turn // 3)) % XS
        return from_reply, owner, from_reply * XS + (1 - from_reply) * owner

    def value_grads(step):
        value = kv[source(step)[2], 1]
        for j in range(HEADS):
            lanes = slice(j * ROWS, (j + 1) * ROWS)
            dps[step, :, lanes] = dot(value, do_t[j]) - rowdots[j, 0:1, :]

    def first_pass(step, carry):
        @pl.when(step == 1)
        def _():
            forward(0)
            forward(1)

        @pl.when(step == 3)
        def _():
            for side in (0, 1):
                x_wait(1, 1 + 2 * side)
                relay_copy(1, side).start()
            for d in range(1, ZS):
                arrived(bias_z.at[(z - d) % ZS], bz_send.at[d], bz_recv.at[d], at_z(d))
            bias_x[x] = (bias_z[0] + bias_z[1]) + (bias_z[2] + bias_z[3])
            for d in range(1, XS):
                bx_copy(d).start()

        @pl.when(step > 0)
        def _():
            value_grads(step - 1)

        @pl.when(step == 2)
        def _():
            for side in (0, 1):
                x_wait(0, 1 + 2 * side)
                relay_copy(0, side).start()

        @pl.when(step == 4)
        def _():
            for side in (0, 1):
                relay_wait(0, side)

        from_reply, owner, block = source(step)
        last = from_reply * query_row + (1 - from_reply) * (prompt_limit - 1 - owner * BLOCK)
        mask[...] = jnp.where(key_row <= last, 0.0, NEGATIVE)
        key = kv[block, 0]
        columns = pl.ds(pl.multiple_of(step * BLOCK, BLOCK), BLOCK)
        keys_t[:, columns] = key.astype(jnp.float32).T.astype(jnp.bfloat16)
        for j in range(HEADS):
            lanes = slice(j * ROWS, (j + 1) * ROWS)
            logits = dot(key, q_t[j]) * to_log2 + mask[...]
            top = jnp.max(logits, axis=0, keepdims=True)
            power = jnp.exp2(logits - top)
            probs[step, :, lanes] = power
            tops[step, j : j + 1, :] = top
            totals[step, j : j + 1, :] = jnp.sum(power, axis=0, keepdims=True)
        return carry

    lax.fori_loop(0, 5, first_pass, 0)

    top = jnp.max(tops[...], axis=0)
    total = jnp.zeros((HEADS, ROWS), jnp.float32)
    for slot in range(5):
        total = total + totals[slot] * jnp.exp2(tops[slot] - top)
    for slot in range(5):
        factors[slot] = jnp.exp2(tops[slot] - top) / total

    for side in (0, 1):
        relay_wait(1, side)
    value_grads(4)

    def second_pass(turn, carry):
        step = 4 - turn
        rows = pl.ds(pl.multiple_of(step * BLOCK, BLOCK), BLOCK)
        for j in range(HEADS):
            lanes = slice(j * ROWS, (j + 1) * ROWS)
            prob = probs[step, :, lanes] * factors[step, j : j + 1, :]
            score = (prob * dps[step, :, lanes]).astype(jnp.bfloat16)
            dscores[rows, lanes] = score
            prob_b[:, lanes] = prob.astype(jnp.bfloat16)
            score_b[:, lanes] = score
        parts[step, 0] = dot(score_b[...], q_st[...]) * scale
        parts[step, 1] = dot(prob_b[...], do_st[...])

        for slot, way in ((4, 2), (3, 3), (2, 1)):
            @pl.when(step == slot)
            def _():
                near_out[way] = parts[slot].astype(jnp.bfloat16)
                for d in (1, 2, 3, 0):
                    near_copy(way, d).start()
                if slot == 2:
                    for d in range(1, XS):
                        arrived(bias_x.at[(x - d) % XS], bx_send.at[d], bx_recv.at[d], at_x(d))
                    bias_y[group] = (bias_x[0] + bias_x[1]) + (bias_x[2] + bias_x[3])
                    for d in range(1, groups):
                        by_copy(d).start()

        @pl.when(step == 1)
        def _():
            for d in (1, 2, 3, 0):
                rows = rows_of(d)
                total = parts[1, :, rows]
                for way in (2, 3, 1):
                    near_wait(way, d)
                    total = total + near_in[way, :, rows].astype(jnp.float32)
                if d == 0:
                    parts[1, :, rows] = total
                else:
                    col_out[:, rows] = total.astype(jnp.bfloat16)
                    col_copy(d).start()

        @pl.when(step == 0)
        def _():
            rg_v[...] = parts[0].astype(jnp.bfloat16)
        return carry

    lax.fori_loop(0, 5, second_pass, 0)
    reply_store = pltpu.make_async_copy(rg_v, rg_hbm.at[0, 0], out_sem.at[0])
    reply_store.start()
    for j in range(HEADS):
        cols = slice(j * HD, (j + 1) * HD)
        lanes = slice(j * ROWS, (j + 1) * ROWS)
        turned = dot(keys_t[...], dscores[:, lanes])
        qg_v[:, cols] = (turned.T * scale).astype(jnp.bfloat16)
    query_store = pltpu.make_async_copy(qg_v, qg_hbm.at[0, 0], out_sem.at[1])
    query_store.start()

    for d in range(1, ZS):
        arrived(col_in.at[d], col_send.at[d], col_recv.at[d], at_z(d))
    for side in (0, 1):
        total = parts[1, side, rows_of(0), :]
        for d in range(1, ZS):
            total = total + col_in[d, side].astype(jnp.float32)
        pg_v[side] = total.astype(jnp.bfloat16)
    prompt_store = pltpu.make_async_copy(pg_v, pg_hbm.at[0], out_sem.at[2])
    prompt_store.start()
    for d in range(1, groups):
        arrived(bias_y.at[(group - d) % groups], by_send.at[d], by_recv.at[d], at_group(d))
    bias_out[...] = jnp.sum(jnp.sum(bias_y[...], axis=0), axis=0, keepdims=True)
    started = [z_copy(kind, d) for kind in (0, 1) for d in range(1, ZS)]
    started += [x_copy(kind, way, d) for kind in (0, 1) for way in x_ways[kind] for d in range(ZS)]
    started += [relay_copy(kind, side) for kind in (0, 1) for side in (0, 1)] + [col_copy(d) for d in range(1, ZS)]
    started += [near_copy(way, d) for way in range(1, XS) for d in range(ZS)]
    started += [bz_copy(d) for d in range(1, ZS)] + [bx_copy(d) for d in range(1, XS)]
    started += [by_copy(d) for d in range(1, groups)]
    for copy in started:
        copy.wait_send()
    reply_store.wait()
    query_store.wait()
    prompt_store.wait()


def hand_over(
    query_in, reply_in, prompt_in, bias_in, query_out, reply_out, prompt_out, bias_out,
    query_v, reply_v, prompt_v, bias_v, in_sem, out_sem,
):
    piece = ROWS // 4
    moves = [
        (query_in.at[0, 0, rows], query_v.at[rows], query_out.at[0, 0, rows])
        for rows in (pl.ds(i * piece, piece) for i in range(4))
    ]
    moves += [(reply_in, reply_v, reply_out), (prompt_in, prompt_v, prompt_out)]
    moves += [(bias_in, bias_v, bias_out)]
    enter = [pltpu.make_async_copy(m[0], m[1], in_sem.at[i]) for i, m in enumerate(moves)]
    leave = [pltpu.make_async_copy(m[1], m[2], out_sem.at[i]) for i, m in enumerate(moves)]
    for copy in enter:
        copy.start()
    for before, after in zip(enter, leave):
        before.wait()
        after.start()
    for copy in leave:
        copy.wait()


def on_device(groups, queries, reply_kv, prompt_kv, saved_out, grad_out, prompt_len, reply_len):
    half, full = jnp.bfloat16, jnp.float32
    vmem = pltpu.VMEM
    dma = pltpu.SemaphoreType.DMA
    anywhere = pl.BlockSpec(memory_space=pl.ANY)
    wide = HEADS * HD
    lanes = HEADS * ROWS
    results = pl.pallas_call(
        functools.partial(kernel, groups),
        out_shape=(
            jax.ShapeDtypeStruct(queries.shape, half),
            jax.ShapeDtypeStruct(reply_kv.shape, half),
            jax.ShapeDtypeStruct(prompt_kv.shape, half),
            jax.ShapeDtypeStruct((1, HD), full),
        ),
        in_specs=[pl.BlockSpec(memory_space=vmem)] * 2 + [anywhere] * 5,
        out_specs=(anywhere, anywhere, anywhere, pl.BlockSpec(memory_space=vmem)),
        scratch_shapes=[
            vmem((ROWS, wide), half),
            vmem((ROWS, wide), half),
            vmem((ROWS, wide), half),
            vmem((lanes, HD), half),
            vmem((lanes, HD), half),
            vmem((HEADS, HD, ROWS), half),
            vmem((HEADS, HD, ROWS), half),
            vmem((XS + 1, 2, BLOCK, HD), half),
            vmem((BLOCK, ROWS), full),
            vmem((5, BLOCK, lanes), full),
            vmem((5, BLOCK, lanes), full),
            vmem((BLOCK, lanes), half),
            vmem((BLOCK, lanes), half),
            vmem((5 * BLOCK, lanes), half),
            vmem((HD, 5 * BLOCK), half),
            vmem((5, HEADS, ROWS), full),
            vmem((5, HEADS, ROWS), full),
            vmem((5, HEADS, ROWS), full),
            vmem((HEADS, 8, ROWS), full),
            vmem((5, 2, BLOCK, HD), full),
            vmem((XS, 2, BLOCK, HD), half),
            vmem((XS, 2, BLOCK, HD), half),
            vmem((2, BLOCK, HD), half),
            vmem((ZS, 2, SLICE, HD), half),
            vmem((ZS, 8, HD), full),
            vmem((XS, 8, HD), full),
            vmem((groups, 8, HD), full),
            vmem((ROWS, wide), half),
            vmem((2, ROWS, HD), half),
            vmem((2, SLICE, HD), half),
            dma((5,)), dma((3,)),
            dma((2, ZS)), dma((2, ZS)), dma((2, XS, ZS)), dma((2, XS, ZS)), dma((2, 2)), dma((2, 2)),
            dma((XS, ZS)), dma((XS, ZS)), dma((ZS,)), dma((ZS,)),
            dma((ZS,)), dma((ZS,)), dma((XS,)), dma((XS,)),
            dma((groups,)), dma((groups,)),
        ],
        compiler_params=pltpu.CompilerParams(
            collective_id=0, has_side_effects=True, vmem_limit_bytes=56 * 2**20
        ),
        cost_estimate=pl.CostEstimate(
            flops=5 * 2 * lanes * 5 * BLOCK * HD,
            bytes_accessed=5 * 2**20,
            transcendentals=lanes * 5 * BLOCK,
        ),
    )(prompt_len.reshape(1, 1), reply_len, queries, reply_kv, prompt_kv, saved_out, grad_out)
    query_grad, reply_grad, prompt_grad, bias = pl.pallas_call(
        hand_over,
        out_shape=tuple(jax.ShapeDtypeStruct(r.shape, r.dtype) for r in results),
        in_specs=[anywhere] * 4,
        out_specs=(anywhere,) * 4,
        scratch_shapes=[
            vmem((ROWS, wide), half),
            vmem(reply_kv.shape, half),
            vmem(prompt_kv.shape, half),
            vmem((1, HD), full),
            dma((7,)),
            dma((7,)),
        ],
        compiler_params=pltpu.CompilerParams(vmem_limit_bytes=60 * 2**20),
    )(*results)
    return query_grad, reply_grad, prompt_grad, bias.reshape(HD)


def solution(mesh):
    in_specs = (
        P("grp", "reply", None, "head"),
        P("grp", "reply", None, None, "head"),
        P("grp", None, "reply", "head"),
        P("grp", "reply", None, "head"),
        P("grp", "reply", None, "head"),
        P("grp"),
        P("grp", "reply"),
    )
    out_specs = (
        P("grp", "reply", None, "head"),
        P("grp", "reply", None, None, "head"),
        P("grp", None, "reply", "head"),
        P("head"),
    )
    return jax.shard_map(
        functools.partial(on_device, mesh.shape["grp"]),
        mesh=mesh, in_specs=in_specs, out_specs=out_specs, check_vma=False,
    )
```

```python
import functools
import math

import jax
import jax.numpy as jnp
from jax import lax
from jax.experimental import pallas as pl
from jax.experimental.pallas import tpu as pltpu
from jax.sharding import PartitionSpec as P

NEGATIVE = -1e30
XS = 4
ZS = 4
HD = 128
HEADS = 8
ROWS = 256
SLICE = 64
BLOCK = ZS * SLICE
NT = (((1,), (1,)), ((), ()))
NN = (((1,), (0,)), ((), ()))


def dot(a, b, dims=NN):
    return lax.dot_general(a, b, dims, preferred_element_type=jnp.float32)


def kernel(
    groups,
    plen_ref, rlen_ref, q_hbm, rkv_hbm, pkv_hbm, o_hbm, do_hbm,
    qg_hbm, rg_hbm, pg_hbm, bias_out,
    q_v, do_v, o_v, q_st, do_st, q_t, do_t, kv, mask, probs, dps, prob_b, score_b, dscores, keys_t,
    tops, totals, factors, rowdots, parts,
    near_out, near_in, col_out, col_in,
    bias_z, bias_x, bias_y, qg_v, rg_v, pg_v,
    local_sem, out_sem, z_send, z_recv, x_send, x_recv, relay_send, relay_recv,
    near_send, near_recv, col_send, col_recv,
    bz_send, bz_recv, bx_send, bx_recv, by_send, by_recv,
):
    group = lax.axis_index("grp")
    reply = lax.axis_index("reply")
    x = reply // ZS
    z = reply % ZS
    scale = HD ** (-0.5)
    to_log2 = scale * math.log2(math.e)

    def at_z(d):
        return {"reply": x * ZS + (z + d) % ZS}

    def at_x(d):
        return {"reply": ((x + d) % XS) * ZS + z}

    def at_group(d):
        return {"grp": (group + d) % groups}

    def remote(src, dst, send, recv, device):
        return pltpu.make_async_remote_copy(
            src_ref=src, dst_ref=dst, send_sem=send, recv_sem=recv,
            device_id=device, device_id_type=pl.DeviceIdType.MESH,
        )

    def arrived(place, send, recv, device):
        remote(place, place, send, recv, device).wait_recv()

    def rows_of(d):
        return pl.ds(pl.multiple_of(((z + d) % ZS) * SLICE, SLICE), SLICE)

    barrier = pltpu.get_barrier_semaphore()
    partners = [at_z(d) for d in range(1, ZS)] + [at_x(d) for d in range(1, XS)]
    partners += [at_group(d) for d in range(1, groups)]
    for device in partners:
        pl.semaphore_signal(barrier, inc=1, device_id=device, device_id_type=pl.DeviceIdType.MESH)

    loads = [
        pltpu.make_async_copy(pkv_hbm.at[0], kv.at[x, :, rows_of(0)], local_sem.at[0]),
        pltpu.make_async_copy(do_hbm.at[0, 0], do_v, local_sem.at[1]),
        pltpu.make_async_copy(o_hbm.at[0, 0], o_v, local_sem.at[2]),
        pltpu.make_async_copy(rkv_hbm.at[0, 0], kv.at[XS], local_sem.at[3]),
        pltpu.make_async_copy(q_hbm.at[0, 0], q_v, local_sem.at[4]),
    ]
    for load in loads:
        load.start()

    def z_copy(kind, d):
        place = kv.at[x, kind, rows_of(0)]
        return remote(place, place, z_send.at[kind, d], z_recv.at[kind, d], at_z(d))

    def z_wait(kind, d):
        arrived(kv.at[x, kind, rows_of(-d)], z_send.at[kind, d], z_recv.at[kind, d], at_z(d))

    def x_copy(kind, way, d):
        place = kv.at[x, kind, rows_of(-d)]
        return remote(place, place, x_send.at[kind, way, d], x_recv.at[kind, way, d], at_x(way))

    def x_wait(kind, way):
        for d in range(ZS):
            arrived(kv.at[(x - way) % XS, kind, rows_of(-d)], x_send.at[kind, way, d],
                    x_recv.at[kind, way, d], at_x(way))

    x_ways = ((1, 3), (1, 3))

    def half_of(side):
        return pl.ds(side * (BLOCK // 2), BLOCK // 2)

    def relay_copy(kind, side):
        way = 1 - 2 * side
        place = kv.at[(x - way) % XS, kind, half_of(side)]
        return remote(place, place, relay_send.at[kind, side], relay_recv.at[kind, side],
                      at_x(way))

    def relay_wait(kind, side):
        arrived(kv.at[(x + 2) % XS, kind, half_of(side)], relay_send.at[kind, side],
                relay_recv.at[kind, side], at_x(1 - 2 * side))

    def near_copy(way, d):
        return remote(near_out.at[way, :, rows_of(d)], near_in.at[way, :, rows_of(d)],
                      near_send.at[way, d], near_recv.at[way, d], at_x(way))

    def near_wait(way, d):
        arrived(near_in.at[way, :, rows_of(d)], near_send.at[way, d], near_recv.at[way, d],
                at_x(way))

    def col_copy(d):
        return remote(col_out.at[:, rows_of(d)], col_in.at[d], col_send.at[d], col_recv.at[d],
                      at_z(d))

    def bz_copy(d):
        return remote(bias_z.at[z], bias_z.at[z], bz_send.at[d], bz_recv.at[d], at_z(d))

    def bx_copy(d):
        return remote(bias_x.at[x], bias_x.at[x], bx_send.at[d], bx_recv.at[d], at_x(d))

    def by_copy(d):
        return remote(bias_y.at[group], bias_y.at[group], by_send.at[d], by_recv.at[d], at_group(d))

    loads[0].wait()
    pl.semaphore_wait(barrier, len(partners))
    for kind in (0, 1):
        for d in range(1, ZS):
            z_copy(kind, d).start()
        for way in x_ways[kind]:
            x_copy(kind, way, 0).start()

    for i in (1, 2):
        loads[i].wait()
    limit = rlen_ref[...]
    live = lax.broadcasted_iota(jnp.int32, (ROWS, HD), 0) < limit
    ones = jnp.ones((8, HD), jnp.bfloat16)
    bias = jnp.zeros((8, HD), jnp.float32)
    for j in range(HEADS):
        cols = slice(j * HD, (j + 1) * HD)
        grad = jnp.where(live, do_v[:, cols].astype(jnp.float32), 0.0)
        do_st[j * ROWS : (j + 1) * ROWS, :] = grad.astype(jnp.bfloat16)
        do_t[j] = grad.T.astype(jnp.bfloat16)
        bias = bias + jnp.sum(grad.reshape(ROWS // 8, 8, HD), axis=0)
        product = grad * o_v[:, cols].astype(jnp.float32)
        high = product.astype(jnp.bfloat16)
        low = (product - high.astype(jnp.float32)).astype(jnp.bfloat16)
        rowdots[j] = dot(ones, high, NT) + dot(ones, low, NT)
    bias_z[z] = bias
    for d in range(1, ZS):
        bz_copy(d).start()

    def forward(kind):
        for d in range(1, ZS):
            z_wait(kind, d)
            for way in x_ways[kind]:
                x_copy(kind, way, d).start()

    for i in (3, 4):
        loads[i].wait()
    for j in range(HEADS):
        query = q_v[:, j * HD : (j + 1) * HD]
        q_st[j * ROWS : (j + 1) * ROWS, :] = query
        q_t[j] = query.astype(jnp.float32).T.astype(jnp.bfloat16)
    prompt_limit = plen_ref[...]
    key_row = lax.broadcasted_iota(jnp.int32, (BLOCK, ROWS), 0)
    query_row = lax.broadcasted_iota(jnp.int32, (BLOCK, ROWS), 1)

    def source(step):
        from_reply = 1 - (step + 3) // 4
        turn = step + 3 - 4 * ((step + 3) // 4)
        owner = (x + turn + turn // 2 - 2 * (turn // 3)) % XS
        return from_reply, owner, from_reply * XS + (1 - from_reply) * owner

    def value_grads(step):
        value = kv[source(step)[2], 1]
        for j in range(HEADS):
            lanes = slice(j * ROWS, (j + 1) * ROWS)
            dps[step, :, lanes] = dot(value, do_t[j]) - rowdots[j, 0:1, :]

    def first_pass(step, carry):
        @pl.when(step == 1)
        def _():
            forward(1)

        @pl.when(step == 3)
        def _():
            for side in (0, 1):
                x_wait(1, 1 + 2 * side)
                relay_copy(1, side).start()
            for d in range(1, ZS):
                arrived(bias_z.at[(z - d) % ZS], bz_send.at[d], bz_recv.at[d], at_z(d))
            bias_x[x] = (bias_z[0] + bias_z[1]) + (bias_z[2] + bias_z[3])
            for d in range(1, XS):
                bx_copy(d).start()

        @pl.when(step > 0)
        def _():
            value_grads(step - 1)

        @pl.when(step == 2)
        def _():
            for side in (0, 1):
                x_wait(0, 1 + 2 * side)
                relay_copy(0, side).start()

        @pl.when(step == 4)
        def _():
            for side in (0, 1):
                relay_wait(0, side)

        from_reply, owner, block = source(step)
        last = from_reply * query_row + (1 - from_reply) * (prompt_limit - 1 - owner * BLOCK)
        mask[...] = jnp.where(key_row <= last, 0.0, NEGATIVE)
        key = kv[block, 0]
        columns = pl.ds(pl.multiple_of(step * BLOCK, BLOCK), BLOCK)
        keys_t[:, columns] = key.astype(jnp.float32).T.astype(jnp.bfloat16)
        for j in range(HEADS):
            lanes = slice(j * ROWS, (j + 1) * ROWS)
            logits = dot(key, q_t[j]) * to_log2 + mask[...]
            top = jnp.max(logits, axis=0, keepdims=True)
            power = jnp.exp2(logits - top)
            probs[step, :, lanes] = power
            tops[step, j : j + 1, :] = top
            totals[step, j : j + 1, :] = jnp.sum(power, axis=0, keepdims=True)
        return carry

    forward(0)
    lax.fori_loop(0, 5, first_pass, 0)

    top = jnp.max(tops[...], axis=0)
    total = jnp.zeros((HEADS, ROWS), jnp.float32)
    for slot in range(5):
        total = total + totals[slot] * jnp.exp2(tops[slot] - top)
    for slot in range(5):
        factors[slot] = jnp.exp2(tops[slot] - top) / total

    for side in (0, 1):
        relay_wait(1, side)
    value_grads(4)

    def second_pass(turn, carry):
        step = 4 - turn
        rows = pl.ds(pl.multiple_of(step * BLOCK, BLOCK), BLOCK)
        for j in range(HEADS):
            lanes = slice(j * ROWS, (j + 1) * ROWS)
            prob = probs[step, :, lanes] * factors[step, j : j + 1, :]
            score = (prob * dps[step, :, lanes]).astype(jnp.bfloat16)
            dscores[rows, lanes] = score
            prob_b[:, lanes] = prob.astype(jnp.bfloat16)
            score_b[:, lanes] = score
        parts[step, 0] = dot(score_b[...], q_st[...]) * scale
        parts[step, 1] = dot(prob_b[...], do_st[...])

        for slot, way in ((4, 2), (3, 3), (2, 1)):
            @pl.when(step == slot)
            def _():
                near_out[way] = parts[slot].astype(jnp.bfloat16)
                for d in (1, 2, 3, 0):
                    near_copy(way, d).start()
                if slot == 2:
                    for d in range(1, XS):
                        arrived(bias_x.at[(x - d) % XS], bx_send.at[d], bx_recv.at[d], at_x(d))
                    bias_y[group] = (bias_x[0] + bias_x[1]) + (bias_x[2] + bias_x[3])
                    for d in range(1, groups):
                        by_copy(d).start()

        @pl.when(step == 1)
        def _():
            for d in (1, 2, 3, 0):
                rows = rows_of(d)
                total = parts[1, :, rows]
                for way in (2, 3, 1):
                    near_wait(way, d)
                    total = total + near_in[way, :, rows].astype(jnp.float32)
                if d == 0:
                    parts[1, :, rows] = total
                else:
                    col_out[:, rows] = total.astype(jnp.bfloat16)
                    col_copy(d).start()

        @pl.when(step == 0)
        def _():
            rg_v[...] = parts[0].astype(jnp.bfloat16)
        return carry

    lax.fori_loop(0, 5, second_pass, 0)
    reply_store = pltpu.make_async_copy(rg_v, rg_hbm.at[0, 0], out_sem.at[0])
    reply_store.start()
    for j in range(HEADS):
        cols = slice(j * HD, (j + 1) * HD)
        lanes = slice(j * ROWS, (j + 1) * ROWS)
        turned = dot(keys_t[...], dscores[:, lanes])
        qg_v[:, cols] = (turned.T * scale).astype(jnp.bfloat16)
    query_store = pltpu.make_async_copy(qg_v, qg_hbm.at[0, 0], out_sem.at[1])
    query_store.start()

    for d in range(1, ZS):
        arrived(col_in.at[d], col_send.at[d], col_recv.at[d], at_z(d))
    for side in (0, 1):
        total = parts[1, side, rows_of(0), :]
        for d in range(1, ZS):
            total = total + col_in[d, side].astype(jnp.float32)
        pg_v[side] = total.astype(jnp.bfloat16)
    prompt_store = pltpu.make_async_copy(pg_v, pg_hbm.at[0], out_sem.at[2])
    prompt_store.start()
    for d in range(1, groups):
        arrived(bias_y.at[(group - d) % groups], by_send.at[d], by_recv.at[d], at_group(d))
    bias_out[...] = jnp.sum(jnp.sum(bias_y[...], axis=0), axis=0, keepdims=True)
    started = [z_copy(kind, d) for kind in (0, 1) for d in range(1, ZS)]
    started += [x_copy(kind, way, d) for kind in (0, 1) for way in x_ways[kind] for d in range(ZS)]
    started += [relay_copy(kind, side) for kind in (0, 1) for side in (0, 1)] + [col_copy(d) for d in range(1, ZS)]
    started += [near_copy(way, d) for way in range(1, XS) for d in range(ZS)]
    started += [bz_copy(d) for d in range(1, ZS)] + [bx_copy(d) for d in range(1, XS)]
    started += [by_copy(d) for d in range(1, groups)]
    for copy in started:
        copy.wait_send()
    reply_store.wait()
    query_store.wait()
    prompt_store.wait()


def hand_over(
    query_in, reply_in, prompt_in, bias_in, query_out, reply_out, prompt_out, bias_out,
    query_v, reply_v, prompt_v, bias_v, in_sem, out_sem,
):
    piece = ROWS // 4
    moves = [
        (query_in.at[0, 0, rows], query_v.at[rows], query_out.at[0, 0, rows])
        for rows in (pl.ds(i * piece, piece) for i in range(4))
    ]
    moves += [(reply_in, reply_v, reply_out), (prompt_in, prompt_v, prompt_out)]
    moves += [(bias_in, bias_v, bias_out)]
    enter = [pltpu.make_async_copy(m[0], m[1], in_sem.at[i]) for i, m in enumerate(moves)]
    leave = [pltpu.make_async_copy(m[1], m[2], out_sem.at[i]) for i, m in enumerate(moves)]
    for copy in enter:
        copy.start()
    for before, after in zip(enter, leave):
        before.wait()
        after.start()
    for copy in leave:
        copy.wait()


def on_device(groups, queries, reply_kv, prompt_kv, saved_out, grad_out, prompt_len, reply_len):
    half, full = jnp.bfloat16, jnp.float32
    vmem = pltpu.VMEM
    dma = pltpu.SemaphoreType.DMA
    anywhere = pl.BlockSpec(memory_space=pl.ANY)
    wide = HEADS * HD
    lanes = HEADS * ROWS
    results = pl.pallas_call(
        functools.partial(kernel, groups),
        out_shape=(
            jax.ShapeDtypeStruct(queries.shape, half),
            jax.ShapeDtypeStruct(reply_kv.shape, half),
            jax.ShapeDtypeStruct(prompt_kv.shape, half),
            jax.ShapeDtypeStruct((1, HD), full),
        ),
        in_specs=[pl.BlockSpec(memory_space=vmem)] * 2 + [anywhere] * 5,
        out_specs=(anywhere, anywhere, anywhere, pl.BlockSpec(memory_space=vmem)),
        scratch_shapes=[
            vmem((ROWS, wide), half),
            vmem((ROWS, wide), half),
            vmem((ROWS, wide), half),
            vmem((lanes, HD), half),
            vmem((lanes, HD), half),
            vmem((HEADS, HD, ROWS), half),
            vmem((HEADS, HD, ROWS), half),
            vmem((XS + 1, 2, BLOCK, HD), half),
            vmem((BLOCK, ROWS), full),
            vmem((5, BLOCK, lanes), full),
            vmem((5, BLOCK, lanes), full),
            vmem((BLOCK, lanes), half),
            vmem((BLOCK, lanes), half),
            vmem((5 * BLOCK, lanes), half),
            vmem((HD, 5 * BLOCK), half),
            vmem((5, HEADS, ROWS), full),
            vmem((5, HEADS, ROWS), full),
            vmem((5, HEADS, ROWS), full),
            vmem((HEADS, 8, ROWS), full),
            vmem((5, 2, BLOCK, HD), full),
            vmem((XS, 2, BLOCK, HD), half),
            vmem((XS, 2, BLOCK, HD), half),
            vmem((2, BLOCK, HD), half),
            vmem((ZS, 2, SLICE, HD), half),
            vmem((ZS, 8, HD), full),
            vmem((XS, 8, HD), full),
            vmem((groups, 8, HD), full),
            vmem((ROWS, wide), half),
            vmem((2, ROWS, HD), half),
            vmem((2, SLICE, HD), half),
            dma((5,)), dma((3,)),
            dma((2, ZS)), dma((2, ZS)), dma((2, XS, ZS)), dma((2, XS, ZS)), dma((2, 2)), dma((2, 2)),
            dma((XS, ZS)), dma((XS, ZS)), dma((ZS,)), dma((ZS,)),
            dma((ZS,)), dma((ZS,)), dma((XS,)), dma((XS,)),
            dma((groups,)), dma((groups,)),
        ],
        compiler_params=pltpu.CompilerParams(
            collective_id=0, has_side_effects=True, vmem_limit_bytes=56 * 2**20
        ),
        cost_estimate=pl.CostEstimate(
            flops=5 * 2 * lanes * 5 * BLOCK * HD,
            bytes_accessed=5 * 2**20,
            transcendentals=lanes * 5 * BLOCK,
        ),
    )(prompt_len.reshape(1, 1), reply_len, queries, reply_kv, prompt_kv, saved_out, grad_out)
    query_grad, reply_grad, prompt_grad, bias = pl.pallas_call(
        hand_over,
        out_shape=tuple(jax.ShapeDtypeStruct(r.shape, r.dtype) for r in results),
        in_specs=[anywhere] * 4,
        out_specs=(anywhere,) * 4,
        scratch_shapes=[
            vmem((ROWS, wide), half),
            vmem(reply_kv.shape, half),
            vmem(prompt_kv.shape, half),
            vmem((1, HD), full),
            dma((7,)),
            dma((7,)),
        ],
        compiler_params=pltpu.CompilerParams(vmem_limit_bytes=60 * 2**20),
    )(*results)
    return query_grad, reply_grad, prompt_grad, bias.reshape(HD)


def solution(mesh):
    in_specs = (
        P("grp", "reply", None, "head"),
        P("grp", "reply", None, None, "head"),
        P("grp", None, "reply", "head"),
        P("grp", "reply", None, "head"),
        P("grp", "reply", None, "head"),
        P("grp"),
        P("grp", "reply"),
    )
    out_specs = (
        P("grp", "reply", None, "head"),
        P("grp", "reply", None, None, "head"),
        P("grp", None, "reply", "head"),
        P("head"),
    )
    return jax.shard_map(
        functools.partial(on_device, mesh.shape["grp"]),
        mesh=mesh, in_specs=in_specs, out_specs=out_specs, check_vma=False,
    )
```
